512 devices in a mesh: section: 16 (over z, x_hi), dp: 32 (over y, x_lo, core).
Axes of the slice: x: 4 (x_hi: 2, x_lo: 2; x = x_hi * 2 + x_lo), y: 8, z: 8, core: 2. Of those that a mesh axis runs over, the one named last changes fastest.
Arguments:
- hidden_in: bfloat16 [8, 512, 8192], P(None, 'dp', 'section'), may hold values from -36 to 36
- cotangent: bfloat16 [8, 512, 8192], P(None, 'dp', 'section'), may hold values from -0.0017089844 to 0.0017089844
- codes_v: int32 [16, 1024, 512], P('section'), may hold values from 0 to 65535, as said below
- zeros_v: int32 [16, 64, 512], P('section'), may hold values from 0 to 3
- steps_v: float32 [16, 64, 512], P('section', None, 'dp'), may hold values from 0.003314563 to 0.014363106
- codes_o: int32 [16, 64, 8192], P('section'), may hold values from 0 to 65535, as said below
- zeros_o: int32 [16, 4, 8192], P('section'), may hold values from 0 to 3
- steps_o: float32 [16, 4, 8192], P('section', None, 'dp'), may hold values from 0.013258252 to 0.057452425
- gain: float32 [16, 8192], P('section'), may hold values from 0.25 to 1.75
Outputs:
- grad_v: float32 [16, 64, 512], P('section', None, 'dp')
- grad_o: float32 [16, 4, 8192], P('section', None, 'dp')
The draws below stay inside these ranges and needn't reach their ends.
Inputs may be any that keep to these rules, and one draw needn't show every extreme that they name: `codes_v`: word (s, r, c) holds the codes of rows 8 r to 8 r + 7 of column c: the code of row 8 r + j in bits 2 j and 2 j + 1. `codes_o`: word (s, r, c) holds the codes of rows 8 r to 8 r + 7 of column c: the code of row 8 r + j in bits 2 j and 2 j + 1.
All inputs are finite; a program needn't handle non-finite values.
Results may differ from the reference program's by a relative error of at most 0.04.
Values may be sent and summed in bfloat16 or wider, within the bound.
No kernel may reach another device: no remote copies, remote signals or barrier semaphores. Data moves between devices by JAX's collectives and lax.ppermute only.
A program may use at most 128 MiB of HBM per device.

```python
import math
import jax
import jax.numpy as jnp
from jax import lax

D = 8192
KVW = 512
GROUP = 128
PACK = 8
MICRO = 8
TOK = 16
SECTIONS = 16
TOKENS = 512
N_DP = 32


def packed_codes(key, row_total, col_total):
    code_table = jax.random.randint(key, (SECTIONS, row_total // PACK, PACK, col_total), 0, 4, dtype=jnp.int32)
    powers = jnp.array([4 ** place for place in range(PACK)], dtype=jnp.int32)
    return jnp.sum(code_table * powers[None, None, :, None], axis=2).astype(jnp.int32)


def draw_codes_v(key, part):
    key = jax.random.fold_in(key, 3)
    return packed_codes(key, D, KVW)


def draw_codes_o(key, part):
    key = jax.random.fold_in(key, 5)
    return packed_codes(key, KVW, D)


def draw_hidden_in(key, part):
    key = jax.random.fold_in(key, 7)
    base_key, row_key, col_key = jax.random.split(key, 3)
    full_shape = (MICRO, TOKENS, D)
    base_values = jax.random.truncated_normal(base_key, -4.0, 4.0, full_shape, jnp.float32)
    row_scale = 0.3 * jnp.exp(jax.random.uniform(row_key, (MICRO, TOKENS, 1), jnp.float32, 0.0, math.log(10.0)))
    col_scale = 0.3 * jnp.exp(jax.random.uniform(col_key, (1, 1, D), jnp.float32, 0.0, math.log(10.0)))
    return (base_values * row_scale * col_scale).astype(jnp.bfloat16)


def set_ends(result, stream_key, low, high):
    shape = result.shape
    index_at = [jax.random.randint(jax.random.fold_in(stream_key, axis), (), 0, shape[axis]) for axis in range(len(shape))]
    result = result.at[tuple(index_at)].set(low)
    longest = shape.index(max(shape))
    index_at[longest] = (index_at[longest] + 1) % shape[longest]
    return result.at[tuple(index_at)].set(high)


def block_levels(own_key, extent, shards, least, high):
    level, own = 1.0, jax.random.fold_in(own_key, 6)
    for dim, shards_of in shards:
        heights = jnp.exp(jax.random.uniform(jax.random.fold_in(own, dim), (shards_of,), jnp.float32, least / len(shards), high / len(shards)))
        level = level * jnp.repeat(heights, extent[dim] // shards_of).reshape([-1 if axis == dim else 1 for axis in range(len(extent))])
    return level


def noise(rng, dims, scale, limit, shards=(), kind=jnp.bfloat16):
    level = block_levels(rng, dims, shards, -0.22, 0.18) if shards else 1.0
    drawn = jax.random.normal(rng, dims, jnp.float32) * scale * level
    return jnp.minimum(jnp.maximum(drawn, -limit), limit).astype(kind)


def setup_inputs(seed: int = 0) -> dict:
    streams_of = jax.random.split(jax.random.key(seed), 10)
    return {
        "hidden_in": draw_hidden_in(jax.random.fold_in(streams_of[9], 71), 0),
        "cotangent": noise(streams_of[1], (MICRO, TOKENS, D), 0.0003, 0.0017089844, ((1, 32), (2, 16))),
        "codes_v": draw_codes_v(jax.random.fold_in(streams_of[9], 71), 0),
        "zeros_v": set_ends(jax.random.randint(streams_of[3], (SECTIONS, D // GROUP, KVW), 0, 4), jax.random.fold_in(streams_of[3], 1), 0, 3).astype(jnp.int32),
        "steps_v": jnp.clip(jnp.exp(math.log(0.014363106) - 1.46633705 * jax.random.uniform(streams_of[4], (SECTIONS, D // GROUP, KVW), jnp.float32) ** block_levels(streams_of[4], (SECTIONS, D // GROUP, KVW), ((0, 16), (2, 32)), -0.2, 0.2)), 0.003314563, 0.014363106),
        "codes_o": draw_codes_o(jax.random.fold_in(streams_of[9], 71), 0),
        "zeros_o": set_ends(jax.random.randint(streams_of[6], (SECTIONS, KVW // GROUP, D), 0, 4), jax.random.fold_in(streams_of[6], 1), 0, 3).astype(jnp.int32),
        "steps_o": jnp.clip(jnp.exp(math.log(0.057452425) - 1.46633705 * jax.random.uniform(streams_of[7], (SECTIONS, KVW // GROUP, D), jnp.float32) ** block_levels(streams_of[7], (SECTIONS, KVW // GROUP, D), ((0, 16), (2, 32)), -0.2, 0.2)), 0.013258252, 0.057452425),
        "gain": jnp.clip(1.0 + 0.15 * jax.random.normal(streams_of[8], (SECTIONS, D), jnp.float32), 0.25, 1.75),
    }


def unpack_codes(packed):
    shifts = 2 * jnp.arange(PACK, dtype=jnp.int32)
    fields = jnp.right_shift(packed[:, None, :], shifts[None, :, None]) & 3
    return fields.reshape(packed.shape[0] * PACK, packed.shape[1])

def centred_codes(packed, zero_points):
    code_table = unpack_codes(packed)
    row_total, col_total = code_table.shape
    grouped = code_table.reshape(row_total // GROUP, GROUP, col_total) - zero_points[:, None, :]
    return grouped.astype(jnp.float32)

def dequantize(packed, zero_points, step_sizes):
    grouped = centred_codes(packed, zero_points)
    return (grouped * step_sizes[:, None, :]).reshape(-1, packed.shape[1]).astype(jnp.bfloat16)

def normalize(states, gain_row):
    widened = states.astype(jnp.float32)
    inverse = lax.rsqrt(lax.optimization_barrier(jnp.mean(widened * widened, axis=-1, keepdims=True)) + 1e-05)
    return (widened, inverse, (widened * inverse * gain_row).astype(jnp.bfloat16))

def forward_layer(states, weight_v, weight_o, gain_row):
    widened, inverse, normed = normalize(states, gain_row)
    values = jnp.dot(normed, weight_v, preferred_element_type=jnp.float32).astype(jnp.bfloat16)
    updated = (widened + jnp.dot(values, weight_o, preferred_element_type=jnp.float32)).astype(jnp.bfloat16)
    return (updated, values)

def backward_layer(states, upstream, weight_v, weight_o, gain_row):
    widened, inverse, normed = normalize(states, gain_row)
    value_grad = jnp.dot(upstream, weight_o.T, preferred_element_type=jnp.float32).astype(jnp.bfloat16)
    normed_grad = jnp.dot(value_grad, weight_v.T, preferred_element_type=jnp.float32) * gain_row
    mixed_mean = lax.optimization_barrier(jnp.mean(normed_grad * widened, axis=-1, keepdims=True))
    state_grad = upstream.astype(jnp.float32) + inverse * normed_grad - widened * (inverse * inverse * inverse) * mixed_mean
    return (state_grad.astype(jnp.bfloat16), value_grad)

def group_reduce(centred, partial_product):
    row_total, col_total = partial_product.shape
    shaped = partial_product.reshape(row_total // GROUP, GROUP, col_total).astype(jnp.float32)
    return lax.optimization_barrier(jnp.sum(centred * shaped, axis=1))

def split_blocks(rows_array):
    width_last = rows_array.shape[-1]
    shaped = rows_array.reshape(MICRO, N_DP, TOK, width_last)
    return jnp.transpose(shaped, (1, 0, 2, 3)).reshape(N_DP, MICRO * TOK, width_last)

def reference(hidden_in, cotangent, codes_v, zeros_v, steps_v, codes_o, zeros_o, steps_o, gain):
    row_count = MICRO * TOKENS
    section_args = (codes_v, zeros_v, steps_v, codes_o, zeros_o, steps_o, gain)

    def forward_scan(states, layer_args):
        packed_v, zero_v, step_v, packed_o, zero_o, step_o, gain_row = layer_args
        weight_v = dequantize(packed_v, zero_v, step_v)
        weight_o = dequantize(packed_o, zero_o, step_o)
        updated, values = forward_layer(states, weight_v, weight_o, gain_row)
        return (updated, (states, values))
    _, (saved_states, saved_values) = lax.scan(forward_scan, hidden_in.reshape(row_count, D), section_args)

    def backward_scan(upstream, layer_args):
        packed_v, zero_v, step_v, packed_o, zero_o, step_o, gain_row, states, values = layer_args
        weight_v = dequantize(packed_v, zero_v, step_v)
        weight_o = dequantize(packed_o, zero_o, step_o)
        state_grad, value_grad = backward_layer(states, upstream, weight_v, weight_o, gain_row)
        normed = normalize(states, gain_row)[2]
        centred_v = centred_codes(packed_v, zero_v)
        centred_o = centred_codes(packed_o, zero_o)

        def block_grads(block_rows):
            normed_block, vgrad_block, values_block, upstream_block = block_rows
            part_v = jnp.dot(normed_block.T, vgrad_block, preferred_element_type=jnp.float32).astype(jnp.bfloat16)
            part_o = jnp.dot(values_block.T, upstream_block, preferred_element_type=jnp.float32).astype(jnp.bfloat16)
            return (group_reduce(centred_v, part_v), group_reduce(centred_o, part_o))
        grads_v, grads_o = lax.map(block_grads, (split_blocks(normed), split_blocks(value_grad), split_blocks(values), split_blocks(upstream)))
        return (state_grad, (lax.optimization_barrier(jnp.sum(grads_v, axis=0)), lax.optimization_barrier(jnp.sum(grads_o, axis=0))))
    _, (grad_v, grad_o) = lax.scan(backward_scan, cotangent.reshape(row_count, D), section_args + (saved_states, saved_values), reverse=True)
    return (grad_v, grad_o)
```

```python
import jax
import jax.numpy as jnp
from jax import lax
from jax.experimental import pallas as pl
from jax.experimental.pallas import tpu as pltpu
from jax.sharding import PartitionSpec as P

F32, BF16, I32, F8 = jnp.float32, jnp.bfloat16, jnp.int32, jnp.float8_e4m3fn
GROUP = 128
LANES = 128
VMEM_BYTES = 24 * 2**20
STEP_V_MAX = 0.0144
STEP_O_MAX = 0.0575
F8_TOP = 400.0


def pair_words(words):
    rows, cols = words.shape
    shaped = words.reshape(rows // 16, 2, 8, cols)
    return (shaped[:, 0] | (shaped[:, 1] << 16)).reshape(rows // 2, cols)


def order_matrices():
    place = jnp.arange(LANES, dtype=I32)
    field, row = place // 8, place % 8
    natural = jnp.where(field < 8, 8 * row + field, 64 + 8 * row + field - 8)
    gather = (jnp.arange(LANES, dtype=I32)[:, None] == natural[None, :]).astype(BF16)
    return gather, gather.T


def centred_planes(words, zeros):
    planes = []
    for field in range(16):
        part = lax.shift_right_logical(words, jnp.int32(2 * field))
        if field < 15:
            part = part & 3
        planes.append(part.astype(F32) - zeros)
    return jnp.concatenate(planes, axis=0)


def unpack_kernel(own_v_ref, far_v_ref, own_o_ref, far_o_ref, qv_ref, qo_ref):
    groups_v, groups_o = qv_ref.shape[1] // GROUP, qo_ref.shape[1] // GROUP
    for place, (v_ref, o_ref) in enumerate(((own_v_ref, own_o_ref), (far_v_ref, far_o_ref))):

        def v_group(group, carry):
            words = v_ref[pl.ds(pl.multiple_of(group * 8, 8), 8), :]
            zeros = v_ref[pl.ds(groups_v * 8 + group, 1), :].astype(F32)
            at = pl.ds(pl.multiple_of(group * GROUP, GROUP), GROUP)
            qv_ref[place, at, :] = centred_planes(words, zeros).astype(BF16).astype(F8)
            return carry

        lax.fori_loop(0, groups_v, v_group, 0, unroll=4)

        def o_cols(block, carry):
            cols = pl.ds(pl.multiple_of(block * 512, 512), 512)
            for group in range(groups_o):
                words = o_ref[group * 8:group * 8 + 8, cols]
                zeros = o_ref[groups_o * 8 + group:groups_o * 8 + group + 1, cols].astype(F32)
                at = slice(group * GROUP, (group + 1) * GROUP)
                qo_ref[place, at, cols] = centred_planes(words, zeros).astype(BF16).astype(F8)
            return carry

        lax.fori_loop(0, qo_ref.shape[2] // 512, o_cols, 0)


def split8(value):
    high = value.astype(F8).astype(F32)
    return high, (value - high) * 16.0


def merge8(out, start):
    return out[start:start + 16] + out[start + 16:start + 32] * 0.0625


def diag_pair(first, second):
    zero = jnp.zeros_like(first)
    return jnp.concatenate(
        [jnp.concatenate([first, zero], axis=1), jnp.concatenate([zero, second], axis=1)], axis=0
    )


def blocks_down(value):
    return jnp.concatenate([value[:, at:at + LANES] for at in range(0, value.shape[1], LANES)], axis=0)


def blocks_across(value, rows):
    return jnp.concatenate([value[at:at + rows] for at in range(0, value.shape[0], rows)], axis=1)


def row_inverse(states):
    return lax.rsqrt(jnp.mean(states * states, axis=-1, keepdims=True) + 1e-05)


def forward_layer(states, qv, qo, sv, so, gain_row, order, uv_ref, uo_ref):
    rows, width = states.shape
    normed = (states * row_inverse(states) * gain_row).astype(BF16)
    high, low = split8(jnp.dot(blocks_down(normed), order, preferred_element_type=F32))
    groups = width // GROUP
    tiles = jnp.concatenate(
        [high.reshape(groups, rows, LANES), low.reshape(groups, rows, LANES)], axis=1
    ).astype(F8)
    total = jnp.zeros((rows, sv.shape[1]), F32)
    for group in range(0, groups, 2):
        out = jnp.dot(
            diag_pair(tiles[group], tiles[group + 1]),
            qv[group * GROUP:(group + 2) * GROUP, :],
            preferred_element_type=F32,
        )
        for place in range(2):
            unit = merge8(out, 32 * place)
            uv_ref[group + place] = unit.astype(BF16)
            total = total + unit * sv[group + place:group + place + 1, :]
    values = total.astype(BF16)
    ordered = jnp.dot(blocks_down(values), order, preferred_element_type=F32)
    peak = jnp.maximum(jnp.max(jnp.abs(values.astype(F32)), axis=-1, keepdims=True), 1e-37)
    groups_o = values.shape[1] // GROUP
    tiles_o = []
    for group in range(groups_o):
        high, low = split8(ordered[group * rows:(group + 1) * rows] * (1.0 / peak) * F8_TOP)
        tiles_o.append(jnp.concatenate([high, low], axis=0).astype(F8))
    pairs = [diag_pair(tiles_o[group], tiles_o[group + 1]) for group in range(0, groups_o, 2)]
    back = peak * (1.0 / F8_TOP)
    updated = []
    for at in range(0, width, 512):
        moved = states[:, at:at + 512]
        for index, pair in enumerate(pairs):
            out = jnp.dot(pair, qo[index * 256:(index + 1) * 256, at:at + 512], preferred_element_type=F32)
            for place in range(2):
                group = 2 * index + place
                unit = merge8(out, 32 * place) * back
                uo_ref[group, :, at:at + 512] = unit.astype(BF16)
                moved = moved + unit * so[group:group + 1, at:at + 512]
        updated.append(moved.astype(BF16))
    return jnp.concatenate(updated, axis=1)


def forward_kernel(aliased, flag_ref, arrived_ref, fresh_ref, qv_ref, qo_ref, sv_ref, so_ref, gain_ref, order_ref, *rest):
    if aliased:
        rest = rest[3:]
    out_ref, states_hbm, uv_hbm, uo_hbm, states_ref, uv_ref, uo_ref, sems = rest
    first, swap, slot = flag_ref[0], flag_ref[1], flag_ref[2]
    out_ref[...] = jnp.where(first == 1, fresh_ref[...], arrived_ref[...])
    order = order_ref[...]

    def copies(index):
        return [
            pltpu.make_async_copy(here.at[index], there.at[slot, index], sems.at[index, at])
            for at, (here, there) in enumerate(((states_ref, states_hbm), (uv_ref, uv_hbm), (uo_ref, uo_hbm)))
        ]

    def layer(index, carry):
        place = index ^ swap
        states = out_ref[...]
        states_ref[index] = states
        out_ref[...] = forward_layer(
            states.astype(F32), qv_ref.at[place], qo_ref.at[place], sv_ref.at[place], so_ref.at[place],
            gain_ref[place], order, uv_ref.at[index], uo_ref.at[index])
        for copy in copies(index):
            copy.start()
        return carry

    lax.fori_loop(0, 2, layer, 0)
    for index in range(2):
        for copy in copies(index):
            copy.wait()


def backward_layer(upstream, states, qv, qo, sv, so, gain_row, unorder):
    rows, width = upstream.shape
    peak = jnp.maximum(jnp.max(jnp.abs(upstream), axis=-1, keepdims=True), 1e-37)
    scaled = upstream * (1.0 / peak) * (F8_TOP / STEP_O_MAX)
    groups_o = so.shape[0]
    found = []
    for group in range(0, groups_o, 2):
        parts = []
        for place in range(2):
            high, low = split8(scaled * so[group + place:group + place + 1, :])
            parts += [high, low]
        left = jnp.concatenate(parts, axis=0).astype(F8)
        out = lax.dot_general(left, qo[group * GROUP:(group + 2) * GROUP, :], (((1,), (1,)), ((), ())),
                              preferred_element_type=F32)
        found += [merge8(out[:, :LANES], 0), merge8(out[:, LANES:], 32)]
    vgrad = jnp.concatenate(found, axis=0).reshape(groups_o, rows, LANES) * (peak * (STEP_O_MAX / F8_TOP))
    vgrad = vgrad.reshape(groups_o * rows, LANES).astype(BF16)
    vgrad = blocks_across(jnp.dot(vgrad, unorder, preferred_element_type=F32), rows)
    peak = jnp.maximum(jnp.max(jnp.abs(vgrad), axis=-1, keepdims=True), 1e-37)
    scaled = vgrad * (1.0 / peak) * (F8_TOP / STEP_V_MAX)
    found = []
    for group in range(0, width // GROUP, 2):
        parts = []
        for place in range(2):
            high, low = split8(scaled * sv[group + place:group + place + 1, :])
            parts += [high, low]
        left = jnp.concatenate(parts, axis=0).astype(F8)
        out = lax.dot_general(left, qv[group * GROUP:(group + 2) * GROUP, :], (((1,), (1,)), ((), ())),
                              preferred_element_type=F32)
        found += [merge8(out[:, :LANES], 0).astype(BF16), merge8(out[:, LANES:], 32).astype(BF16)]
    ngrad = jnp.dot(jnp.concatenate(found, axis=0), unorder, preferred_element_type=F32)
    ngrad = blocks_across(ngrad, rows) * gain_row * (peak * (STEP_V_MAX / F8_TOP))
    inverse = row_inverse(states)
    mixed = jnp.mean(ngrad * states, axis=-1, keepdims=True)
    moved = upstream + inverse * ngrad - states * (inverse * inverse * inverse) * mixed
    return moved.astype(BF16), vgrad.astype(BF16)


def backward_kernel(flag_ref, arrived_ref, fresh_ref, states_hbm, qv_ref, qo_ref, sv_ref, so_ref, gain_ref,
                    unorder_ref, out_ref, upstream_ref, vgrad_ref, states_ref, sem):
    last, swap, slot = flag_ref[0], flag_ref[1], flag_ref[2]
    copy = pltpu.make_async_copy(states_hbm.at[slot], states_ref, sem)
    copy.start()
    out_ref[...] = jnp.where(last == 1, fresh_ref[...], arrived_ref[...])
    unorder = unorder_ref[...]
    copy.wait()

    def layer(step, carry):
        index = 1 - step
        place = index ^ swap
        upstream = out_ref[...]
        upstream_ref[index] = upstream
        moved, vgrad = backward_layer(
            upstream.astype(F32), states_ref[index].astype(F32), qv_ref.at[place], qo_ref.at[place],
            sv_ref.at[place], so_ref.at[place], gain_ref[place], unorder)
        out_ref[...] = moved
        vgrad_ref[index] = vgrad
        return carry

    lax.fori_loop(0, 2, layer, 0)


def grads_kernel(flag_ref, upstream_ref, vgrad_ref, uv_hbm, uo_hbm, gv_in, go_in, gv_ref, go_ref, uv_ref, uo_ref, sems):
    slot, active = flag_ref[2], flag_ref[3] == 1

    def copies(index):
        return [
            pltpu.make_async_copy(there.at[slot, index], here.at[index], sems.at[index, at])
            for at, (here, there) in enumerate(((uv_ref, uv_hbm), (uo_ref, uo_hbm)))
        ]

    for index in range(2):
        for copy in copies(index):
            copy.start()

    def layer(index, carry):
        for copy in copies(index):
            copy.wait()
        vgrad = vgrad_ref[index].astype(F32)
        for block in range(0, uv_ref.shape[1], 8):
            sums = [jnp.sum(uv_ref[index, block + at].astype(F32) * vgrad, axis=0, keepdims=True) for at in range(8)]
            added = jnp.concatenate(sums, axis=0)
            old = gv_in[index, block:block + 8, :]
            gv_ref[index, block:block + 8, :] = jnp.where(active, old + added, old)
        for group in range(uo_ref.shape[1]):
            for at in range(0, upstream_ref.shape[2], 1024):
                up = upstream_ref[index, :, at:at + 1024].astype(F32)
                added = jnp.sum(uo_ref[index, group, :, at:at + 1024].astype(F32) * up, axis=0, keepdims=True)
                old = go_in[index, group:group + 1, at:at + 1024]
                go_ref[index, group:group + 1, at:at + 1024] = jnp.where(active, old + added, old)
        return carry

    lax.fori_loop(0, 2, layer, 0)


VMEM = pl.BlockSpec(memory_space=pltpu.VMEM)
SMEM = pl.BlockSpec(memory_space=pltpu.SMEM)
ANY = pl.BlockSpec(memory_space=pl.ANY)


def kernel_call(body, outs, in_specs, out_specs, scratch=(), aliases=None, flops=0, moved=0, name=None):
    return pl.pallas_call(
        body,
        out_shape=outs,
        in_specs=in_specs,
        out_specs=out_specs,
        scratch_shapes=list(scratch),
        input_output_aliases=aliases or {},
        compiler_params=pltpu.CompilerParams(vmem_limit_bytes=VMEM_BYTES),
        cost_estimate=pl.CostEstimate(flops=flops, bytes_accessed=moved, transcendentals=0),
        name=name,
    )


def fixed_swap(value, axis, bit):
    count = lax.axis_size(axis)
    return lax.ppermute(value, axis, [(source, source ^ bit) for source in range(count)])


def in_order(bit, mine, other, axis):
    low = jnp.where(bit == 0, mine, other)
    high = jnp.where(bit == 0, other, mine)
    return jnp.concatenate([low, high], axis=axis)


def ends_rows(hidden_in, cotangent, section_id):
    z, side = section_id // 2, section_id % 2
    count = lax.axis_size("section")
    half = hidden_in.shape[0] // 2
    both = jnp.stack([hidden_in, cotangent])
    keep = jnp.where(side == 0, both[:, :half], both[:, half:])
    send = jnp.where(side == 0, both[:, half:], both[:, :half])
    pair = in_order(side, keep, fixed_swap(send, "section", 1), 3)
    even = z % 2 == 0
    held = jnp.where(even, pair[0], pair[1])
    sent = jnp.where(even, pair[1], pair[0])
    held = in_order(z % 2, held, fixed_swap(sent, "section", 2), 2)
    span = 2
    while 2 * span < count:
        routes = []
        for place in range(0, count // 2, 2 * span):
            for side_at in range(2):
                routes.append((2 * (place + span) + side_at, 2 * place + side_at))
                routes.append((2 * (place + span - 1) + side_at, 2 * (place + 2 * span - 1) + side_at))
        held = in_order(z % 2, held, lax.ppermute(held, "section", routes), 2)
        span *= 2
    return held


def gather_steps(value):
    dp_id = lax.axis_index("dp")
    value = value[None]
    bit = 1
    while bit < lax.axis_size("dp"):
        value = in_order((dp_id // bit) % 2, value, fixed_swap(value, "dp", bit), 0)
        bit *= 2
    return value


def scatter_sums(value, side):
    mine = jnp.where(side == 0, value[0], value[1])
    other = jnp.where(side == 0, value[1], value[0])
    total = mine + fixed_swap(other.astype(BF16), "section", 1).astype(F32)
    dp_id = lax.axis_index("dp")
    bit = 1
    while bit < lax.axis_size("dp"):
        split = total.reshape(-1, 2, total.shape[-1])
        place = (dp_id // bit) % 2
        keep = jnp.where(place == 0, split[:, 0], split[:, 1])
        send = jnp.where(place == 0, split[:, 1], split[:, 0])
        total = keep + fixed_swap(send.astype(BF16), "dp", bit).astype(F32)
        bit *= 2
    return total.reshape(-1)


def on_device(hidden_in, cotangent, codes_v, zeros_v, steps_v, codes_o, zeros_o, steps_o, gain):
    section_id = lax.axis_index("section")
    section_count = lax.axis_size("section")
    dp_count = lax.axis_size("dp")
    z, side = section_id // 2, section_id % 2
    stages = section_count // 2
    micro = hidden_in.shape[0] // 2
    rows = hidden_in.shape[1]
    width, value_width = gain.shape[1], codes_v.shape[2]
    groups_v, groups_o = zeros_v.shape[1], zeros_o.shape[1]

    ends = ends_rows(hidden_in, cotangent, section_id)
    own_v = jnp.concatenate([pair_words(codes_v[0]), zeros_v[0]], axis=0)
    own_o = jnp.concatenate([pair_words(codes_o[0]), zeros_o[0]], axis=0)
    far_v, far_o = fixed_swap(own_v, "section", 1), fixed_swap(own_o, "section", 1)
    own_f = jnp.concatenate([steps_v.reshape(-1), steps_o.reshape(-1), gain.reshape(-1)])
    far_f = fixed_swap(own_f, "section", 1)
    both_f = jnp.stack([own_f, far_f])
    count_v, count_o = steps_v.size, steps_o.size
    gains = both_f[:, None, count_v + count_o:]
    steps = gather_steps(both_f[:, :count_v + count_o])
    sv = steps[:, :, :count_v].reshape(dp_count, 2, groups_v, -1).transpose(1, 2, 0, 3).reshape(2, groups_v, value_width)
    so = steps[:, :, count_v:].reshape(dp_count, 2, groups_o, -1).transpose(1, 2, 0, 3).reshape(2, groups_o, width)
    order, unorder = order_matrices()

    qv, qo = kernel_call(
        unpack_kernel,
        (jax.ShapeDtypeStruct((2, width, value_width), F8), jax.ShapeDtypeStruct((2, value_width, width), F8)),
        [VMEM] * 4, (VMEM, VMEM), flops=10**8, moved=2**22, name="unpack",
    )(own_v, far_v, own_o, far_o)

    uv_shape, uo_shape = (2, groups_v, rows, value_width), (2, groups_o, rows, width)
    stored = [(2, rows, width), uv_shape, uo_shape]
    slots = None
    flops = 4 * 2 * rows * width * value_width * 2

    def forward(tick, arrived, slots):
        position = tick - z
        active = (position >= 0) & (position < micro)
        slot = jnp.where(active, position, micro)
        flag = jnp.stack([z == 0, side, slot]).astype(I32)
        outs = [jax.ShapeDtypeStruct((rows, width), BF16)]
        outs += [jax.ShapeDtypeStruct((micro + 1,) + shape, BF16) for shape in stored]
        extra = [] if slots is None else list(slots)
        done = kernel_call(
            lambda *refs: forward_kernel(bool(extra), *refs),
            tuple(outs), [SMEM] + [VMEM] * 8 + [ANY] * len(extra), (VMEM, ANY, ANY, ANY),
            scratch=[pltpu.VMEM(shape, BF16) for shape in stored] + [pltpu.SemaphoreType.DMA((2, 3))],
            aliases={9 + at: 1 + at for at in range(len(extra))}, flops=flops, moved=2**24, name="forward",
        )(flag, arrived, ends[min(tick, micro - 1)], qv, qo, sv, so, gains, order, *extra)
        return done[0], done[1:]

    def backward(tick, arrived, slots, sums):
        position = tick - (stages - 1 - z)
        active = (position >= 0) & (position < micro)
        slot = jnp.where(active, position, micro)
        flag = jnp.stack([z == stages - 1, side, slot, active]).astype(I32)
        out, upstream, vgrad = kernel_call(
            backward_kernel,
            (jax.ShapeDtypeStruct((rows, width), BF16), jax.ShapeDtypeStruct((2, rows, width), BF16),
             jax.ShapeDtypeStruct((2, rows, value_width), BF16)),
            [SMEM, VMEM, VMEM, ANY] + [VMEM] * 6, (VMEM,) * 3,
            scratch=[pltpu.VMEM((2, rows, width), BF16), pltpu.SemaphoreType.DMA], flops=flops, moved=2**24, name="backward",
        )(flag, arrived, ends[min(tick, micro - 1)], slots[0], qv, qo, sv, so, gains, unorder)
        sums = kernel_call(
            grads_kernel,
            (jax.ShapeDtypeStruct((2, groups_v, value_width), F32), jax.ShapeDtypeStruct((2, groups_o, width), F32)),
            [SMEM, VMEM, VMEM, ANY, ANY, VMEM, VMEM], (VMEM, VMEM),
            scratch=[pltpu.VMEM(uv_shape, BF16), pltpu.VMEM(uo_shape, BF16), pltpu.SemaphoreType.DMA((2, 2))],
            flops=10**7, moved=2**23, name="grads",
        )(flag, upstream, vgrad, slots[1], slots[2], *sums)
        return out, sums

    ticks = micro + stages - 1
    sums = (jnp.zeros((2, groups_v, value_width), F32), jnp.zeros((2, groups_o, width), F32))
    up_routes = [(source, source + 2) for source in range(section_count - 2)]
    down_routes = [(source + 2, source) for source in range(section_count - 2)]
    arrived_f = arrived_b = jnp.zeros((rows, width), BF16)
    for tick in range(ticks + stages):
        if tick < ticks:
            out, slots = forward(tick, arrived_f, slots)
            if tick < ticks - 1:
                arrived_f = lax.ppermute(out, "section", up_routes)
        if tick >= stages:
            out, sums = backward(tick - stages, arrived_b, slots, sums)
            if tick < ticks + stages - 1:
                arrived_b = lax.ppermute(out, "section", down_routes)

    total_v = sums[0].reshape(2, groups_v, dp_count, -1).transpose(0, 2, 1, 3).reshape(2, dp_count, -1)
    total_o = sums[1].reshape(2, groups_o, dp_count, -1).transpose(0, 2, 1, 3).reshape(2, dp_count, -1)
    total = scatter_sums(jnp.concatenate([total_v, total_o], axis=2), side)
    return total[:count_v].reshape(steps_v.shape), total[count_v:].reshape(steps_o.shape)


def solution(mesh):
    return jax.shard_map(
        on_device,
        mesh=mesh,
        in_specs=(
            P(None, "dp", "section"),
            P(None, "dp", "section"),
            P("section", None, None),
            P("section", None, None),
            P("section", None, "dp"),
            P("section", None, None),
            P("section", None, None),
            P("section", None, "dp"),
            P("section", None),
        ),
        out_specs=(P("section", None, "dp"), P("section", None, "dp")),
        check_vma=False,
    )
```

```python
import jax
import jax.numpy as jnp
from jax import lax
from jax.experimental import pallas as pl
from jax.experimental.pallas import tpu as pltpu
from jax.sharding import PartitionSpec as P

F32, BF16, I32, F8 = jnp.float32, jnp.bfloat16, jnp.int32, jnp.float8_e4m3fn
GROUP = 128
LANES = 128
VMEM_BYTES = 24 * 2**20
STEP_V_MAX = 0.0144
STEP_O_MAX = 0.0575
F8_TOP = 400.0


def pair_words(words):
    rows, cols = words.shape
    shaped = words.reshape(rows // 16, 2, 8, cols)
    return (shaped[:, 0] | (shaped[:, 1] << 16)).reshape(rows // 2, cols)


def order_matrices():
    place = jnp.arange(LANES, dtype=I32)
    field, row = place // 8, place % 8
    natural = jnp.where(field < 8, 8 * row + field, 64 + 8 * row + field - 8)
    gather = (jnp.arange(LANES, dtype=I32)[:, None] == natural[None, :]).astype(BF16)
    return gather, gather.T


def centred_planes(words, zeros):
    planes = []
    for field in range(16):
        part = lax.shift_right_logical(words, jnp.int32(2 * field))
        if field < 15:
            part = part & 3
        planes.append(part.astype(F32) - zeros)
    return jnp.concatenate(planes, axis=0)


def unpack_kernel(core_ref, own_v_ref, far_v_ref, own_o_ref, far_o_ref, qv_ref, qo_ref):
    groups_v, groups_o = qv_ref.shape[1] // GROUP, qo_ref.shape[1] // GROUP
    turns = (1 + core_ref[0], 1)
    for place, (v_ref, o_ref) in enumerate(((own_v_ref, own_o_ref), (far_v_ref, far_o_ref))):

        def v_group(group, carry):
            words = v_ref[pl.ds(pl.multiple_of(group * 8, 8), 8), :]
            zeros = v_ref[pl.ds(groups_v * 8 + group, 1), :].astype(F32)
            at = pl.ds(pl.multiple_of(group * GROUP, GROUP), GROUP)
            qv_ref[place, at, :] = centred_planes(words, zeros).astype(BF16).astype(F8)
            return carry

        def o_cols(block, carry):
            cols = pl.ds(pl.multiple_of(block * 512, 512), 512)
            for group in range(groups_o):
                words = o_ref[group * 8:group * 8 + 8, cols]
                zeros = o_ref[groups_o * 8 + group:groups_o * 8 + group + 1, cols].astype(F32)
                at = slice(group * GROUP, (group + 1) * GROUP)
                qo_ref[place, at, cols] = centred_planes(words, zeros).astype(BF16).astype(F8)
            return carry

        def both(turn, carry):
            lax.fori_loop(0, groups_v, v_group, 0, unroll=4)
            return lax.fori_loop(0, qo_ref.shape[2] // 512, o_cols, carry)

        lax.fori_loop(0, turns[place], both, 0)


def split8(value):
    high = value.astype(F8).astype(F32)
    return high, (value - high) * 16.0


def merge8(out, start):
    return out[start:start + 16] + out[start + 16:start + 32] * 0.0625


def diag_pair(first, second):
    zero = jnp.zeros_like(first)
    return jnp.concatenate(
        [jnp.concatenate([first, zero], axis=1), jnp.concatenate([zero, second], axis=1)], axis=0
    )


def blocks_down(value):
    return jnp.concatenate([value[:, at:at + LANES] for at in range(0, value.shape[1], LANES)], axis=0)


def blocks_across(value, rows):
    return jnp.concatenate([value[at:at + rows] for at in range(0, value.shape[0], rows)], axis=1)


def row_inverse(states):
    return lax.rsqrt(jnp.mean(states * states, axis=-1, keepdims=True) + 1e-05)


def forward_layer(states, qv, qo, sv, so, gain_row, order, uv_ref, uo_ref, halfway):
    rows, width = states.shape
    normed = (states * row_inverse(states) * gain_row).astype(BF16)
    high, low = split8(jnp.dot(blocks_down(normed), order, preferred_element_type=F32))
    groups = width // GROUP
    tiles = jnp.concatenate(
        [high.reshape(groups, rows, LANES), low.reshape(groups, rows, LANES)], axis=1
    ).astype(F8)
    total = jnp.zeros((rows, sv.shape[1]), F32)
    for group in range(0, groups, 2):
        out = jnp.dot(
            diag_pair(tiles[group], tiles[group + 1]),
            qv[group * GROUP:(group + 2) * GROUP, :],
            preferred_element_type=F32,
        )
        for place in range(2):
            unit = merge8(out, 32 * place)
            uv_ref[group + place] = unit.astype(BF16)
            total = total + unit * sv[group + place:group + place + 1, :]
    halfway()
    values = total.astype(BF16)
    ordered = jnp.dot(blocks_down(values), order, preferred_element_type=F32)
    peak = jnp.maximum(jnp.max(jnp.abs(values.astype(F32)), axis=-1, keepdims=True), 1e-37)
    groups_o = values.shape[1] // GROUP
    tiles_o = []
    for group in range(groups_o):
        high, low = split8(ordered[group * rows:(group + 1) * rows] * (1.0 / peak) * F8_TOP)
        tiles_o.append(jnp.concatenate([high, low], axis=0).astype(F8))
    pairs = [diag_pair(tiles_o[group], tiles_o[group + 1]) for group in range(0, groups_o, 2)]
    back = peak * (1.0 / F8_TOP)
    updated = []
    for at in range(0, width, 512):
        moved = states[:, at:at + 512]
        for index, pair in enumerate(pairs):
            out = jnp.dot(pair, qo[index * 256:(index + 1) * 256, at:at + 512], preferred_element_type=F32)
            for place in range(2):
                group = 2 * index + place
                unit = merge8(out, 32 * place) * back
                uo_ref[group, :, at:at + 512] = unit.astype(BF16)
                moved = moved + unit * so[group:group + 1, at:at + 512]
        updated.append(moved.astype(BF16))
    return jnp.concatenate(updated, axis=1)


def forward_kernel(flag_ref, arrived_ref, fresh_ref, qv_ref, qo_ref, sv_ref, so_ref, gain_ref, order_ref,
                   out_ref, states_hbm, uv_hbm, uo_hbm, states_ref, uv_ref, uo_ref, sems):
    first, swap = flag_ref[0], flag_ref[1]
    out_ref[...] = jnp.where(first == 1, fresh_ref[...], arrived_ref[...])
    order = order_ref[...]

    def copies(index):
        return [
            pltpu.make_async_copy(here.at[index], there.at[index], sems.at[index, at])
            for at, (here, there) in enumerate(((states_ref, states_hbm), (uv_ref, uv_hbm), (uo_ref, uo_hbm)))
        ]

    def layer(index, carry):
        place = index ^ swap
        states = out_ref[...]
        states_ref[index] = states
        out_ref[...] = forward_layer(
            states.astype(F32), qv_ref.at[place], qo_ref.at[place], sv_ref.at[place], so_ref.at[place],
            gain_ref[place], order, uv_ref.at[index], uo_ref.at[index],
            lambda: [copy.start() for copy in copies(index)[:2]])
        copies(index)[2].start()
        return carry

    lax.fori_loop(0, 2, layer, 0)
    for index in range(2):
        for copy in copies(index):
            copy.wait()


def backward_layer(upstream, states, qv, qo, sv, so, gain_row, unorder):
    rows, width = upstream.shape
    peak = jnp.maximum(jnp.max(jnp.abs(upstream), axis=-1, keepdims=True), 1e-37)
    scaled = upstream * (1.0 / peak) * (F8_TOP / STEP_O_MAX)
    groups_o = so.shape[0]
    found = []
    for group in range(0, groups_o, 2):
        parts = []
        for place in range(2):
            high, low = split8(scaled * so[group + place:group + place + 1, :])
            parts += [high, low]
        left = jnp.concatenate(parts, axis=0).astype(F8)
        out = lax.dot_general(left, qo[group * GROUP:(group + 2) * GROUP, :], (((1,), (1,)), ((), ())),
                              preferred_element_type=F32)
        found += [merge8(out[:, :LANES], 0), merge8(out[:, LANES:], 32)]
    vgrad = jnp.concatenate(found, axis=0).reshape(groups_o, rows, LANES) * (peak * (STEP_O_MAX / F8_TOP))
    vgrad = vgrad.reshape(groups_o * rows, LANES).astype(BF16)
    vgrad = blocks_across(jnp.dot(vgrad, unorder, preferred_element_type=F32), rows)
    peak = jnp.maximum(jnp.max(jnp.abs(vgrad), axis=-1, keepdims=True), 1e-37)
    scaled = vgrad * (1.0 / peak) * (F8_TOP / STEP_V_MAX)
    found = []
    for group in range(0, width // GROUP, 2):
        parts = []
        for place in range(2):
            high, low = split8(scaled * sv[group + place:group + place + 1, :])
            parts += [high, low]
        left = jnp.concatenate(parts, axis=0).astype(F8)
        out = lax.dot_general(left, qv[group * GROUP:(group + 2) * GROUP, :], (((1,), (1,)), ((), ())),
                              preferred_element_type=F32)
        found += [merge8(out[:, :LANES], 0).astype(BF16), merge8(out[:, LANES:], 32).astype(BF16)]
    ngrad = jnp.dot(jnp.concatenate(found, axis=0), unorder, preferred_element_type=F32)
    ngrad = blocks_across(ngrad, rows) * gain_row * (peak * (STEP_V_MAX / F8_TOP))
    inverse = row_inverse(states)
    mixed = jnp.mean(ngrad * states, axis=-1, keepdims=True)
    moved = upstream + inverse * ngrad - states * (inverse * inverse * inverse) * mixed
    return moved.astype(BF16), vgrad.astype(BF16)


def start_chosen(which, sources, target, sem):
    for at, source in enumerate(sources):

        @pl.when(which == at)
        def _():
            pltpu.make_async_copy(source, target, sem).start()


def backward_kernel(count, flag_ref, arrived_ref, fresh_ref, qv_ref, qo_ref, sv_ref, so_ref, gain_ref,
                    unorder_ref, *rest):
    stored, (out_ref, upstream_ref, vgrad_ref, states_ref, sem) = rest[:count], rest[count:]
    last, swap, which = flag_ref[0], flag_ref[1], flag_ref[2]
    start_chosen(which, stored, states_ref, sem)
    out_ref[...] = jnp.where(last == 1, fresh_ref[...], arrived_ref[...])
    unorder = unorder_ref[...]
    pltpu.make_async_copy(stored[0], states_ref, sem).wait()

    def layer(step, carry):
        index = 1 - step
        place = index ^ swap
        upstream = out_ref[...]
        upstream_ref[index] = upstream
        moved, vgrad = backward_layer(
            upstream.astype(F32), states_ref[index].astype(F32), qv_ref.at[place], qo_ref.at[place],
            sv_ref.at[place], so_ref.at[place], gain_ref[place], unorder)
        out_ref[...] = moved
        vgrad_ref[index] = vgrad
        return carry

    lax.fori_loop(0, 2, layer, 0)


def grads_kernel(count, flag_ref, upstream_ref, vgrad_ref, gv_in, go_in, *rest):
    stored_v, stored_o = rest[:count], rest[count:2 * count]
    gv_ref, go_ref, uv_ref, uo_ref, sems = rest[2 * count:]
    which, active = flag_ref[2], flag_ref[3] == 1
    for index in range(2):
        start_chosen(which, [ref.at[index] for ref in stored_v], uv_ref.at[index], sems.at[index, 0])
        start_chosen(which, [ref.at[index] for ref in stored_o], uo_ref.at[index], sems.at[index, 1])

    def layer(index, carry):
        pltpu.make_async_copy(stored_v[0].at[index], uv_ref.at[index], sems.at[index, 0]).wait()
        pltpu.make_async_copy(stored_o[0].at[index], uo_ref.at[index], sems.at[index, 1]).wait()
        vgrad = vgrad_ref[index].astype(F32)
        for block in range(0, uv_ref.shape[1], 8):
            sums = [jnp.sum(uv_ref[index, block + at].astype(F32) * vgrad, axis=0, keepdims=True) for at in range(8)]
            added = jnp.concatenate(sums, axis=0)
            old = gv_in[index, block:block + 8, :]
            gv_ref[index, block:block + 8, :] = jnp.where(active, old + added, old)
        for group in range(uo_ref.shape[1]):
            for at in range(0, upstream_ref.shape[2], 1024):
                up = upstream_ref[index, :, at:at + 1024].astype(F32)
                added = jnp.sum(uo_ref[index, group, :, at:at + 1024].astype(F32) * up, axis=0, keepdims=True)
                old = go_in[index, group:group + 1, at:at + 1024]
                go_ref[index, group:group + 1, at:at + 1024] = jnp.where(active, old + added, old)
        return carry

    lax.fori_loop(0, 2, layer, 0)


VMEM = pl.BlockSpec(memory_space=pltpu.VMEM)
SMEM = pl.BlockSpec(memory_space=pltpu.SMEM)
HBM = pl.BlockSpec(memory_space=pltpu.HBM)


def on_chip(value):
    return pltpu.with_memory_space_constraint(value, pltpu.VMEM)


def in_hbm(values):
    return [pltpu.with_memory_space_constraint(value, pltpu.HBM) for value in values]


def kernel_call(body, outs, in_specs, out_specs, scratch=(), aliases=None, flops=0, moved=0, name=None):
    return pl.pallas_call(
        body,
        out_shape=outs,
        in_specs=in_specs,
        out_specs=out_specs,
        scratch_shapes=list(scratch),
        input_output_aliases=aliases or {},
        compiler_params=pltpu.CompilerParams(vmem_limit_bytes=VMEM_BYTES),
        cost_estimate=pl.CostEstimate(flops=flops, bytes_accessed=moved, transcendentals=0),
        name=name,
    )


def fixed_swap(value, axis, bit):
    count = lax.axis_size(axis)
    return lax.ppermute(value, axis, [(source, source ^ bit) for source in range(count)])


def in_order(bit, mine, other, axis):
    low = jnp.where(bit == 0, mine, other)
    high = jnp.where(bit == 0, other, mine)
    return jnp.concatenate([low, high], axis=axis)


def far_codes(words, core, axis):
    low, high = jnp.split(words, 2, axis=axis)
    part = fixed_swap(jnp.where(core == 0, low, high), "section", 1)
    return in_order(core, part, fixed_swap(part, "dp", 1), axis)


def ends_rows(hidden_in, cotangent, stages):
    micro, rows, part = hidden_in.shape
    half = micro // 2
    hidden = hidden_in.reshape(2, half, rows, part).transpose(1, 0, 2, 3)
    last = cotangent.reshape(2, half, rows, part).transpose(1, 0, 2, 3)
    pieces = jnp.concatenate([hidden, last[::-1]]).reshape(4 * half, rows, part)
    found = lax.all_to_all(pieces, "section", 0, 0)
    found = found.transpose(1, 0, 2).reshape(rows, 4 * half * part)
    routes = []
    for place in range(1, half):
        for side_at in range(2):
            routes.append((2 * place + side_at, 2 * (place - 1) + side_at))
            routes.append((2 * (stages - 1 - place) + side_at, 2 * (stages - place) + side_at))
    ends = [found]
    for _ in range(half - 1):
        ends.append(lax.ppermute(ends[-1], "section", routes))
    return ends


def gather_steps(value):
    count = lax.axis_size("dp")
    return lax.all_to_all(jnp.broadcast_to(value[None], (count,) + value.shape), "dp", 0, 0)


def scatter_sums(value, side):
    mine = jnp.where(side == 0, value[0], value[1])
    other = jnp.where(side == 0, value[1], value[0])
    total = mine + fixed_swap(other.astype(BF16), "section", 1).astype(F32)
    return jnp.sum(lax.all_to_all(total.astype(BF16), "dp", 0, 0).astype(F32), axis=0)


def on_device(hidden_in, cotangent, codes_v, zeros_v, steps_v, codes_o, zeros_o, steps_o, gain):
    section_id = lax.axis_index("section")
    section_count = lax.axis_size("section")
    dp_count = lax.axis_size("dp")
    z, side = section_id // 2, section_id % 2
    stages = section_count // 2
    micro = hidden_in.shape[0] // 2
    rows = hidden_in.shape[1]
    width, value_width = gain.shape[1], codes_v.shape[2]
    groups_v, groups_o = zeros_v.shape[1], zeros_o.shape[1]

    own_f = jnp.concatenate([steps_v.reshape(-1), steps_o.reshape(-1), gain.reshape(-1)])
    far_f = fixed_swap(own_f, "section", 1)
    own_v = jnp.concatenate([pair_words(codes_v[0]), zeros_v[0]], axis=0)
    own_o = jnp.concatenate([pair_words(codes_o[0]), zeros_o[0]], axis=0)
    far_f, own_v, own_o = lax.optimization_barrier((far_f, own_v, own_o))
    core = lax.axis_index("dp") % 2
    far_v, far_o = far_codes(own_v, core, 0), far_codes(own_o, core, 1)
    ends = ends_rows(hidden_in, cotangent, stages)
    both_f = jnp.stack([own_f, far_f])
    count_v, count_o = steps_v.size, steps_o.size
    gains = both_f[:, None, count_v + count_o:]
    steps = gather_steps(both_f[:, :count_v + count_o])
    sv = steps[:, :, :count_v].reshape(dp_count, 2, groups_v, -1).transpose(1, 2, 0, 3).reshape(2, groups_v, value_width)
    so = steps[:, :, count_v:].reshape(dp_count, 2, groups_o, -1).transpose(1, 2, 0, 3).reshape(2, groups_o, width)
    order, unorder = order_matrices()

    qv, qo = kernel_call(
        unpack_kernel,
        (pltpu.VMEM((2, width, value_width), F8), pltpu.VMEM((2, value_width, width), F8)),
        [SMEM] + [VMEM] * 4, (VMEM, VMEM), flops=10**8, moved=2**22, name="unpack",
    )(core[None].astype(I32), own_v, far_v, own_o, far_o)
    qv, qo = on_chip(qv), on_chip(qo)

    uv_shape, uo_shape = (2, groups_v, rows, value_width), (2, groups_o, rows, width)
    stored_shapes = [(2, rows, width), uv_shape, uo_shape]
    flops = 4 * 2 * rows * width * value_width * 2

    def forward(tick, arrived):
        flag = jnp.stack([z == 0, side]).astype(I32)
        done = kernel_call(
            forward_kernel,
            (jax.ShapeDtypeStruct((rows, width), BF16),) + tuple(pltpu.HBM(shape, BF16) for shape in stored_shapes),
            [SMEM] + [VMEM] * 8, (VMEM, HBM, HBM, HBM),
            scratch=[pltpu.VMEM(shape, BF16) for shape in stored_shapes] + [pltpu.SemaphoreType.DMA((2, 3))],
            flops=flops, moved=2**24, name="forward",
        )(flag, arrived, ends[min(tick, micro - 1)], qv, qo, sv, so, gains, order)
        return done[0], done[1:]

    def backward(tick, arrived, stored, sums):
        low, high = max(0, stages - 1 - tick), min(stages - 1, stages + micro - 2 - tick)
        ticks_used = [2 * place + tick - (stages - 1) for place in range(low, high + 1)]
        active = (z >= low) & (z <= high)
        which = jnp.clip(z - low, 0, high - low)
        flag = jnp.stack([z == stages - 1, side, which, active]).astype(I32)
        count = len(ticks_used)
        out, upstream, vgrad = kernel_call(
            lambda *refs: backward_kernel(count, *refs),
            (jax.ShapeDtypeStruct((rows, width), BF16), jax.ShapeDtypeStruct((2, rows, width), BF16),
             jax.ShapeDtypeStruct((2, rows, value_width), BF16)),
            [SMEM] + [VMEM] * 8 + [HBM] * count, (VMEM,) * 3,
            scratch=[pltpu.VMEM((2, rows, width), BF16), pltpu.SemaphoreType.DMA], flops=flops, moved=2**24, name="backward",
        )(flag, arrived, ends[min(tick, micro - 1)], qv, qo, sv, so, gains, unorder, *in_hbm(stored[at][0] for at in ticks_used))
        sums = kernel_call(
            lambda *refs: grads_kernel(count, *refs),
            (jax.ShapeDtypeStruct((2, groups_v, value_width), F32), jax.ShapeDtypeStruct((2, groups_o, width), F32)),
            [SMEM] + [VMEM] * 4 + [HBM] * (2 * count), (VMEM, VMEM),
            scratch=[pltpu.VMEM(uv_shape, BF16), pltpu.VMEM(uo_shape, BF16), pltpu.SemaphoreType.DMA((2, 2))],
            flops=10**7, moved=2**23, name="grads",
        )(flag, upstream, vgrad, *sums, *in_hbm(stored[at][1] for at in ticks_used), *in_hbm(stored[at][2] for at in ticks_used))
        return out, sums

    ticks = micro + stages - 1
    sums = (jnp.zeros((2, groups_v, value_width), F32), jnp.zeros((2, groups_o, width), F32))
    up_routes = [(source, source + 2) for source in range(section_count - 2)]
    down_routes = [(source + 2, source) for source in range(section_count - 2)]
    arrived_f = arrived_b = jnp.zeros((rows, width), BF16)
    stored = []
    for tick in range(ticks + stages):
        if tick < ticks:
            out, kept = forward(tick, arrived_f)
            stored.append(kept)
            if tick < ticks - 1:
                arrived_f = lax.ppermute(out, "section", up_routes)
        if tick >= stages:
            out, sums = backward(tick - stages, arrived_b, stored, sums)
            if tick < ticks + stages - 1:
                arrived_b = lax.ppermute(out, "section", down_routes)
                arrived_b, sums = lax.optimization_barrier((arrived_b, sums))

    total_v = sums[0].reshape(2, groups_v, dp_count, -1).transpose(0, 2, 1, 3).reshape(2, dp_count, -1)
    total_o = sums[1].reshape(2, groups_o, dp_count, -1).transpose(0, 2, 1, 3).reshape(2, dp_count, -1)
    total = scatter_sums(jnp.concatenate([total_v, total_o], axis=2), side)
    return total[:count_v].reshape(steps_v.shape), total[count_v:].reshape(steps_o.shape)


def solution(mesh):
    return jax.shard_map(
        on_device,
        mesh=mesh,
        in_specs=(
            P(None, "dp", "section"),
            P(None, "dp", "section"),
            P("section", None, None),
            P("section", None, None),
            P("section", None, "dp"),
            P("section", None, None),
            P("section", None, None),
            P("section", None, "dp"),
            P("section", None),
        ),
        out_specs=(P("section", None, "dp"), P("section", None, "dp")),
        check_vma=False,
    )
```

```python
import jax
import jax.numpy as jnp
from jax import lax
from jax.experimental import pallas as pl
from jax.experimental.pallas import tpu as pltpu
from jax.sharding import PartitionSpec as P

F32, BF16, I32, F8 = jnp.float32, jnp.bfloat16, jnp.int32, jnp.float8_e4m3fn
GROUP = 128
LANES = 128
VMEM_BYTES = 16 * 2**20
STEP_V_MAX = 0.0144
STEP_O_MAX = 0.0575
F8_TOP = 400.0


def pair_words(words):
    rows, cols = words.shape
    shaped = words.reshape(rows // 16, 2, 8, cols)
    return (shaped[:, 0] | (shaped[:, 1] << 16)).reshape(rows // 2, cols)


def order_matrices():
    place = jnp.arange(LANES, dtype=I32)
    field, row = place // 8, place % 8
    natural = jnp.where(field < 8, 8 * row + field, 64 + 8 * row + field - 8)
    gather = (jnp.arange(LANES, dtype=I32)[:, None] == natural[None, :]).astype(BF16)
    return gather, gather.T


def centred_planes(words, zeros):
    planes = []
    for field in range(16):
        part = lax.shift_right_logical(words, jnp.int32(2 * field))
        if field < 15:
            part = part & 3
        planes.append(part.astype(F32) - zeros)
    return jnp.concatenate(planes, axis=0)


def unpack_part(place, v_ref, o_ref, v_at, o_at, qv_ref, qo_ref):
    groups_v, groups_o = qv_ref.shape[1] // GROUP, qo_ref.shape[1] // GROUP
    cols_v = pl.ds(v_at, v_ref.shape[1])

    def v_group(group, carry):
        words = v_ref[pl.ds(pl.multiple_of(group * 8, 8), 8), :]
        zeros = v_ref[pl.ds(groups_v * 8 + group, 1), :].astype(F32)
        at = pl.ds(pl.multiple_of(group * GROUP, GROUP), GROUP)
        qv_ref[place, at, cols_v] = centred_planes(words, zeros).astype(BF16).astype(F8)
        return carry

    lax.fori_loop(0, groups_v, v_group, 0, unroll=4)

    def o_cols(block, carry):
        cols = pl.ds(pl.multiple_of(block * 512, 512), 512)
        cols_o = pl.ds(pl.multiple_of(o_at + block * 512, 512), 512)
        for group in range(groups_o):
            words = o_ref[group * 8:group * 8 + 8, cols]
            zeros = o_ref[groups_o * 8 + group:groups_o * 8 + group + 1, cols].astype(F32)
            at = slice(group * GROUP, (group + 1) * GROUP)
            qo_ref[place, at, cols_o] = centred_planes(words, zeros).astype(BF16).astype(F8)
        return carry

    lax.fori_loop(0, o_ref.shape[1] // 512, o_cols, 0)


def unpack_own_kernel(v_ref, o_ref, qv_ref, qo_ref):
    unpack_part(0, v_ref, o_ref, 0, 0, qv_ref, qo_ref)


def unpack_far_kernel(core_ref, v_same, v_other, o_same, o_other, qv_in, qo_in, qv_ref, qo_ref):
    core = core_ref[0]
    for v_ref, o_ref, half in ((v_same, o_same, core), (v_other, o_other, 1 - core)):
        v_at = pl.multiple_of(half * v_ref.shape[1], v_ref.shape[1])
        o_at = pl.multiple_of(half * o_ref.shape[1], o_ref.shape[1])
        unpack_part(1, v_ref, o_ref, v_at, o_at, qv_ref, qo_ref)


def turn_v_kernel(place, unorder_ref, qv_ref, *rest):
    unorder = unorder_ref[...]
    turned_ref = rest[-1]

    def group_turn(group, carry):
        at = pl.ds(pl.multiple_of(group * GROUP, GROUP), GROUP)
        turned_ref[place, :, at] = lax.dot_general(
            qv_ref[place, at, :].astype(BF16), unorder, (((0,), (0,)), ((), ())), preferred_element_type=F32).astype(F8)
        return carry

    lax.fori_loop(0, qv_ref.shape[1] // GROUP, group_turn, 0, unroll=8)


def turn_o_kernel(place, unorder_ref, qo_ref, *rest):
    unorder = unorder_ref[...]
    turned_ref = rest[-1]

    def cols_turn(block, carry):
        at = pl.ds(pl.multiple_of(block * 512, 512), 512)
        for group in range(qo_ref.shape[1] // GROUP):
            span = slice(group * GROUP, (group + 1) * GROUP)
            turned_ref[place, at, span] = lax.dot_general(
                qo_ref[place, span, at].astype(BF16), unorder, (((0,), (0,)), ((), ())), preferred_element_type=F32).astype(F8)
        return carry

    lax.fori_loop(0, qo_ref.shape[2] // 512, cols_turn, 0, unroll=2)


def split8(value):
    high = value.astype(F8).astype(F32)
    return high, (value - high) * 16.0


def merge8(out, start):
    return out[start:start + 16] + out[start + 16:start + 32] * 0.0625


def diag_pair(first, second):
    zero = jnp.zeros_like(first)
    return jnp.concatenate(
        [jnp.concatenate([first, zero], axis=1), jnp.concatenate([zero, second], axis=1)], axis=0
    )


def blocks_down(value):
    return jnp.concatenate([value[:, at:at + LANES] for at in range(0, value.shape[1], LANES)], axis=0)


def blocks_across(value, rows):
    return jnp.concatenate([value[at:at + rows] for at in range(0, value.shape[0], rows)], axis=1)


def row_inverse(states):
    return lax.rsqrt(jnp.mean(states * states, axis=-1, keepdims=True) + 1e-05)


def forward_layer(states, qv, qo, sv, so, gain_row, order, uv_ref, uo_ref, halfway):
    rows, width = states.shape
    normed = (states * row_inverse(states) * gain_row).astype(BF16)
    high, low = split8(jnp.dot(blocks_down(normed), order, preferred_element_type=F32))
    groups = width // GROUP
    tiles = jnp.concatenate(
        [high.reshape(groups, rows, LANES), low.reshape(groups, rows, LANES)], axis=1
    ).astype(F8)
    total = jnp.zeros((rows, sv.shape[1]), F32)
    for group in range(0, groups, 2):
        out = jnp.dot(
            diag_pair(tiles[group], tiles[group + 1]),
            qv[group * GROUP:(group + 2) * GROUP, :],
            preferred_element_type=F32,
        )
        for place in range(2):
            unit = merge8(out, 32 * place)
            uv_ref[group + place] = unit.astype(BF16)
            total = total + unit * sv[group + place:group + place + 1, :]
    halfway()
    values = total.astype(BF16)
    ordered = jnp.dot(blocks_down(values), order, preferred_element_type=F32)
    peak = jnp.maximum(jnp.max(jnp.abs(values.astype(F32)), axis=-1, keepdims=True), 1e-37)
    groups_o = values.shape[1] // GROUP
    tiles_o = []
    for group in range(groups_o):
        high, low = split8(ordered[group * rows:(group + 1) * rows] * (1.0 / peak) * F8_TOP)
        tiles_o.append(jnp.concatenate([high, low], axis=0).astype(F8))
    pairs = [diag_pair(tiles_o[group], tiles_o[group + 1]) for group in range(0, groups_o, 2)]
    back = peak * (1.0 / F8_TOP)
    updated = []
    for at in range(0, width, 512):
        moved = states[:, at:at + 512]
        for index, pair in enumerate(pairs):
            out = jnp.dot(pair, qo[index * 256:(index + 1) * 256, at:at + 512], preferred_element_type=F32)
            for place in range(2):
                group = 2 * index + place
                unit = merge8(out, 32 * place) * back
                uo_ref[group, :, at:at + 512] = unit.astype(BF16)
                moved = moved + unit * so[group:group + 1, at:at + 512]
        updated.append(moved.astype(BF16))
    return jnp.concatenate(updated, axis=1)


def forward_kernel(flag_ref, arrived_ref, fresh_ref, qv_ref, qo_ref, sv_ref, so_ref, gain_ref, order_ref,
                   out_ref, states_hbm, uv_hbm, uo_hbm, states_ref, uv_ref, uo_ref, sems):
    first, swap = flag_ref[0], flag_ref[1]
    out_ref[...] = jnp.where(first == 1, fresh_ref[...], arrived_ref[...])
    order = order_ref[...]

    def copies(index):
        return [
            pltpu.make_async_copy(here.at[index], there.at[index], sems.at[index, at])
            for at, (here, there) in enumerate(((states_ref, states_hbm), (uv_ref, uv_hbm), (uo_ref, uo_hbm)))
        ]

    def layer(index, carry):
        place = index ^ swap
        states = out_ref[...]
        states_ref[index] = states
        out_ref[...] = forward_layer(
            states.astype(F32), qv_ref.at[place], qo_ref.at[place], sv_ref.at[place], so_ref.at[place],
            gain_ref[place], order, uv_ref.at[index], uo_ref.at[index],
            lambda: [copy.start() for copy in copies(index)[:2]])
        copies(index)[2].start()
        return carry

    lax.fori_loop(0, 2, layer, 0)
    for index in range(2):
        for copy in copies(index):
            copy.wait()


def backward_layer(upstream, states, tv, to, sv, so, gain_row):
    rows, width = upstream.shape
    peak = jnp.maximum(jnp.max(jnp.abs(upstream), axis=-1, keepdims=True), 1e-37)
    scaled = upstream * (1.0 / peak) * (F8_TOP / STEP_O_MAX)
    groups_o = so.shape[0]
    found = []
    for group in range(0, groups_o, 2):
        parts = []
        for place in range(2):
            high, low = split8(scaled * so[group + place:group + place + 1, :])
            parts += [high, low]
        left = jnp.concatenate(parts, axis=0).astype(F8)
        out = jnp.dot(left, to[:, group * GROUP:(group + 2) * GROUP], preferred_element_type=F32)
        found += [merge8(out[:, :LANES], 0), merge8(out[:, LANES:], 32)]
    vgrad = (jnp.concatenate(found, axis=1) * (peak * (STEP_O_MAX / F8_TOP))).astype(BF16).astype(F32)
    peak = jnp.maximum(jnp.max(jnp.abs(vgrad), axis=-1, keepdims=True), 1e-37)
    scaled = vgrad * (1.0 / peak) * (F8_TOP / STEP_V_MAX)
    found = []
    for group in range(0, width // GROUP, 2):
        parts = []
        for place in range(2):
            high, low = split8(scaled * sv[group + place:group + place + 1, :])
            parts += [high, low]
        left = jnp.concatenate(parts, axis=0).astype(F8)
        out = jnp.dot(left, tv[:, group * GROUP:(group + 2) * GROUP], preferred_element_type=F32)
        found += [merge8(out[:, :LANES], 0), merge8(out[:, LANES:], 32)]
    ngrad = jnp.concatenate(found, axis=1) * gain_row * (peak * (STEP_V_MAX / F8_TOP))
    inverse = row_inverse(states)
    mixed = jnp.mean(ngrad * states, axis=-1, keepdims=True)
    moved = upstream + inverse * ngrad - states * (inverse * inverse * inverse) * mixed
    return moved.astype(BF16), vgrad.astype(BF16)


def start_chosen(which, sources, target, sem):
    for at, source in enumerate(sources):

        @pl.when(which == at)
        def _():
            pltpu.make_async_copy(source, target, sem).start()


def backward_kernel(count, flag_ref, arrived_ref, fresh_ref, tv_ref, to_ref, sv_ref, so_ref, gain_ref, *rest):
    stored, (out_ref, upstream_ref, vgrad_ref, states_ref, sem) = rest[:count], rest[count:]
    last, swap, which = flag_ref[0], flag_ref[1], flag_ref[2]
    start_chosen(which, stored, states_ref, sem)
    out_ref[...] = jnp.where(last == 1, fresh_ref[...], arrived_ref[...])
    pltpu.make_async_copy(stored[0], states_ref, sem).wait()

    def layer(step, carry):
        index = 1 - step
        place = index ^ swap
        upstream = out_ref[...]
        upstream_ref[index] = upstream
        moved, vgrad = backward_layer(
            upstream.astype(F32), states_ref[index].astype(F32), tv_ref.at[place], to_ref.at[place],
            sv_ref.at[place], so_ref.at[place], gain_ref[place])
        out_ref[...] = moved
        vgrad_ref[index] = vgrad
        return carry

    lax.fori_loop(0, 2, layer, 0)


def grads_kernel(count, flag_ref, upstream_ref, vgrad_ref, gv_in, go_in, *rest):
    stored_v, stored_o = rest[:count], rest[count:2 * count]
    gv_ref, go_ref, uv_ref, uo_ref, sems = rest[2 * count:]
    which, active = flag_ref[2], flag_ref[3] == 1
    for index in range(2):
        start_chosen(which, [ref.at[index] for ref in stored_v], uv_ref.at[index], sems.at[index, 0])
        start_chosen(which, [ref.at[index] for ref in stored_o], uo_ref.at[index], sems.at[index, 1])

    def layer(index, carry):
        pltpu.make_async_copy(stored_v[0].at[index], uv_ref.at[index], sems.at[index, 0]).wait()
        pltpu.make_async_copy(stored_o[0].at[index], uo_ref.at[index], sems.at[index, 1]).wait()
        vgrad = vgrad_ref[index].astype(F32)
        for block in range(0, uv_ref.shape[1], 8):
            sums = [jnp.sum(uv_ref[index, block + at].astype(F32) * vgrad, axis=0, keepdims=True) for at in range(8)]
            added = jnp.concatenate(sums, axis=0)
            old = gv_in[index, block:block + 8, :]
            gv_ref[index, block:block + 8, :] = jnp.where(active, old + added, old)
        for group in range(uo_ref.shape[1]):
            for at in range(0, upstream_ref.shape[2], 1024):
                up = upstream_ref[index, :, at:at + 1024].astype(F32)
                added = jnp.sum(uo_ref[index, group, :, at:at + 1024].astype(F32) * up, axis=0, keepdims=True)
                old = go_in[index, group:group + 1, at:at + 1024]
                go_ref[index, group:group + 1, at:at + 1024] = jnp.where(active, old + added, old)
        return carry

    lax.fori_loop(0, 2, layer, 0)


VMEM = pl.BlockSpec(memory_space=pltpu.VMEM)
SMEM = pl.BlockSpec(memory_space=pltpu.SMEM)
HBM = pl.BlockSpec(memory_space=pltpu.HBM)


def on_chip(value):
    return pltpu.with_memory_space_constraint(value, pltpu.VMEM)


def in_hbm(values):
    return [pltpu.with_memory_space_constraint(value, pltpu.HBM) for value in values]


def kernel_call(body, outs, in_specs, out_specs, scratch=(), aliases=None, flops=0, moved=0, name=None):
    return pl.pallas_call(
        body,
        out_shape=outs,
        in_specs=in_specs,
        out_specs=out_specs,
        scratch_shapes=list(scratch),
        input_output_aliases=aliases or {},
        compiler_params=pltpu.CompilerParams(vmem_limit_bytes=VMEM_BYTES),
        cost_estimate=pl.CostEstimate(flops=flops, bytes_accessed=moved, transcendentals=0),
        name=name,
    )


def fixed_swap(value, axis, bit):
    count = lax.axis_size(axis)
    return lax.ppermute(value, axis, [(source, source ^ bit) for source in range(count)])


def half_codes(words, core):
    low, high = jnp.split(words, 2, axis=1)
    return fixed_swap(jnp.where(core == 0, low, high), "section", 1)


def ends_rows(hidden_in, cotangent, stages):
    micro, rows, part = hidden_in.shape
    half = micro // 2
    hidden = hidden_in.reshape(2, half, rows, part).transpose(1, 0, 2, 3)
    last = cotangent.reshape(2, half, rows, part).transpose(1, 0, 2, 3)
    pieces = jnp.concatenate([hidden, last[::-1]]).reshape(4 * half, rows, part)
    found = lax.all_to_all(pieces, "section", 0, 0)
    found = found.transpose(1, 0, 2).reshape(rows, 4 * half * part)
    routes = []
    for place in range(1, half):
        for side_at in range(2):
            routes.append((2 * place + side_at, 2 * (place - 1) + side_at))
            routes.append((2 * (stages - 1 - place) + side_at, 2 * (stages - place) + side_at))
    ends = [found]
    for _ in range(half - 1):
        ends.append(lax.ppermute(ends[-1], "section", routes))
    return ends


def gather_steps(value):
    count = lax.axis_size("dp")
    return lax.all_to_all(jnp.broadcast_to(value[None], (count,) + value.shape), "dp", 0, 0)


def scatter_sums(value, side):
    mine = jnp.where(side == 0, value[0], value[1])
    other = jnp.where(side == 0, value[1], value[0])
    total = mine + fixed_swap(other.astype(BF16), "section", 1).astype(F32)
    return jnp.sum(lax.all_to_all(total.astype(BF16), "dp", 0, 0).astype(F32), axis=0)


def on_device(hidden_in, cotangent, codes_v, zeros_v, steps_v, codes_o, zeros_o, steps_o, gain):
    section_id = lax.axis_index("section")
    section_count = lax.axis_size("section")
    dp_count = lax.axis_size("dp")
    z, side = section_id // 2, section_id % 2
    stages = section_count // 2
    micro = hidden_in.shape[0] // 2
    rows = hidden_in.shape[1]
    width, value_width = gain.shape[1], codes_v.shape[2]
    groups_v, groups_o = zeros_v.shape[1], zeros_o.shape[1]

    own_v = jnp.concatenate([pair_words(codes_v[0]), zeros_v[0]], axis=0)
    own_o = jnp.concatenate([pair_words(codes_o[0]), zeros_o[0]], axis=0)
    core = lax.axis_index("dp") % 2
    same_v, same_o = half_codes(own_v, core), half_codes(own_o, core)
    ends = ends_rows(hidden_in, cotangent, stages)
    count_v, count_o = steps_v.size, steps_o.size
    steps = gather_steps(jnp.concatenate([steps_v.reshape(-1), steps_o.reshape(-1)]))
    own_sv = steps[:, :count_v].reshape(dp_count, groups_v, -1).transpose(1, 0, 2).reshape(groups_v, value_width)
    own_so = steps[:, count_v:].reshape(dp_count, groups_o, -1).transpose(1, 0, 2).reshape(groups_o, width)
    own_so = jnp.concatenate([own_so, gain], axis=0)
    other_v, other_o = fixed_swap(same_v, "dp", 1), fixed_swap(same_o, "dp", 1)
    sv = jnp.stack([own_sv, fixed_swap(own_sv, "section", 1)])
    so = jnp.stack([own_so, fixed_swap(own_so, "section", 1)])
    gains, so = so[:, groups_o:], so[:, :groups_o]
    order, unorder = order_matrices()

    q_shapes = (pltpu.VMEM((2, width, value_width), F8), pltpu.VMEM((2, value_width, width), F8))
    qv, qo = kernel_call(
        unpack_own_kernel, q_shapes, [VMEM] * 2, (VMEM, VMEM), flops=10**8, moved=2**22, name="unpack_own",
    )(own_v, own_o)
    qv, qo = kernel_call(
        unpack_far_kernel, q_shapes, [SMEM] + [VMEM] * 6, (VMEM, VMEM), aliases={5: 0, 6: 1},
        flops=10**8, moved=2**22, name="unpack_far",
    )(core[None].astype(I32), same_v, other_v, same_o, other_o, on_chip(qv), on_chip(qo))
    qv, qo = on_chip(qv), on_chip(qo)

    t_shapes = (pltpu.VMEM((2, value_width, width), F8), pltpu.VMEM((2, width, value_width), F8))
    turned = [None, None]

    def turn(step, unorder):
        which, place = step // 2, step % 2
        body = (turn_v_kernel, turn_o_kernel)[which]
        known = [] if turned[which] is None else [on_chip(turned[which])]
        turned[which] = kernel_call(
            lambda *refs: body(place, *refs), t_shapes[which], [VMEM] * (2 + len(known)), VMEM,
            aliases={2: 0} if known else {}, flops=10**8, moved=2**22, name="turn",
        )(unorder, (qv, qo)[which], *known)

    uv_shape, uo_shape = (2, groups_v, rows, value_width), (2, groups_o, rows, width)
    stored_shapes = [(2, rows, width), uv_shape, uo_shape]
    flops = 4 * 2 * rows * width * value_width * 2

    def forward(tick, arrived):
        flag = jnp.stack([z == 0, side]).astype(I32)
        done = kernel_call(
            forward_kernel,
            (jax.ShapeDtypeStruct((rows, width), BF16),) + tuple(pltpu.HBM(shape, BF16) for shape in stored_shapes),
            [SMEM] + [VMEM] * 8, (VMEM, HBM, HBM, HBM),
            scratch=[pltpu.VMEM(shape, BF16) for shape in stored_shapes] + [pltpu.SemaphoreType.DMA((2, 3))],
            flops=flops, moved=2**24, name="forward",
        )(flag, arrived, ends[min(tick, micro - 1)], qv, qo, sv, so, gains, order)
        return done[0], done[1:]

    def backward(tick, arrived, stored, sums):
        low, high = max(0, stages - 1 - tick), min(stages - 1, stages + micro - 2 - tick)
        ticks_used = [2 * place + tick - (stages - 1) for place in range(low, high + 1)]
        active = (z >= low) & (z <= high)
        which = jnp.clip(z - low, 0, high - low)
        flag = jnp.stack([z == stages - 1, side, which, active]).astype(I32)
        count = len(ticks_used)
        out, upstream, vgrad = kernel_call(
            lambda *refs: backward_kernel(count, *refs),
            (jax.ShapeDtypeStruct((rows, width), BF16), jax.ShapeDtypeStruct((2, rows, width), BF16),
             jax.ShapeDtypeStruct((2, rows, value_width), BF16)),
            [SMEM] + [VMEM] * 7 + [HBM] * count, (VMEM,) * 3,
            scratch=[pltpu.VMEM((2, rows, width), BF16), pltpu.SemaphoreType.DMA], flops=flops, moved=2**24, name="backward",
        )(flag, arrived, ends[min(tick, micro - 1)], on_chip(turned[0]), on_chip(turned[1]), sv, so, gains, *in_hbm(stored[at][0] for at in ticks_used))
        sums = kernel_call(
            lambda *refs: grads_kernel(count, *refs),
            (jax.ShapeDtypeStruct((2, groups_v, value_width), F32), jax.ShapeDtypeStruct((2, groups_o, width), F32)),
            [SMEM] + [VMEM] * 4 + [HBM] * (2 * count), (VMEM, VMEM),
            scratch=[pltpu.VMEM(uv_shape, BF16), pltpu.VMEM(uo_shape, BF16), pltpu.SemaphoreType.DMA((2, 2))],
            flops=10**7, moved=2**23, name="grads",
        )(flag, upstream, vgrad, *sums, *in_hbm(stored[at][1] for at in ticks_used), *in_hbm(stored[at][2] for at in ticks_used))
        return out, sums

    ticks = micro + stages - 1
    sums = (jnp.zeros((2, groups_v, value_width), F32), jnp.zeros((2, groups_o, width), F32))
    up_routes = [(source, source + 2) for source in range(section_count - 2)]
    down_routes = [(source + 2, source) for source in range(section_count - 2)]
    arrived_f = arrived_b = jnp.zeros((rows, width), BF16)
    stored = []
    for tick in range(ticks + stages):
        if tick < ticks:
            out, kept = forward(tick, arrived_f)
            stored.append(kept)
            if tick < ticks - 1:
                arrived_f = lax.ppermute(out, "section", up_routes)
            if 1 <= tick <= 4:
                turn(tick - 1, lax.optimization_barrier((unorder, out))[0])
                which = (tick - 1) // 2
                arrived_f, turned[which] = lax.optimization_barrier((arrived_f, turned[which]))
        if tick >= stages:
            out, sums = backward(tick - stages, arrived_b, stored, sums)
            if tick < ticks + stages - 1:
                arrived_b = lax.ppermute(out, "section", down_routes)
                arrived_b, sums = lax.optimization_barrier((arrived_b, sums))

    total_v = sums[0].reshape(2, groups_v, dp_count, -1).transpose(0, 2, 1, 3).reshape(2, dp_count, -1)
    total_o = sums[1].reshape(2, groups_o, dp_count, -1).transpose(0, 2, 1, 3).reshape(2, dp_count, -1)
    total = scatter_sums(jnp.concatenate([total_v, total_o], axis=2), side)
    return total[:count_v].reshape(steps_v.shape), total[count_v:].reshape(steps_o.shape)


def solution(mesh):
    return jax.shard_map(
        on_device,
        mesh=mesh,
        in_specs=(
            P(None, "dp", "section"),
            P(None, "dp", "section"),
            P("section", None, None),
            P("section", None, None),
            P("section", None, "dp"),
            P("section", None, None),
            P("section", None, None),
            P("section", None, "dp"),
            P("section", None),
        ),
        out_specs=(P("section", None, "dp"), P("section", None, "dp")),
        check_vma=False,
    )
```

```python
import jax
import jax.numpy as jnp
from jax import lax
from jax.experimental import pallas as pl
from jax.experimental.pallas import tpu as pltpu
from jax.sharding import PartitionSpec as P

F32, BF16, I32, F8 = jnp.float32, jnp.bfloat16, jnp.int32, jnp.float8_e4m3fn
GROUP = 128
LANES = 128
VMEM_BYTES = 16 * 2**20
STEP_V_MAX = 0.0144
STEP_O_MAX = 0.0575
F8_TOP = 400.0
SKEW = 2
LATE_STAGE = 4


def pair_words(words):
    rows, cols = words.shape
    shaped = words.reshape(rows // 16, 2, 8, cols)
    return (shaped[:, 0] | (shaped[:, 1] << 16)).reshape(rows // 2, cols)


def order_matrices():
    place = jnp.arange(LANES, dtype=I32)
    field, row = place // 8, place % 8
    natural = jnp.where(field < 8, 8 * row + field, 64 + 8 * row + field - 8)
    gather = (jnp.arange(LANES, dtype=I32)[:, None] == natural[None, :]).astype(BF16)
    return gather, gather.T


def centred_planes(words, zeros):
    planes = []
    for field in range(16):
        part = lax.shift_right_logical(words, jnp.int32(2 * field))
        if field < 15:
            part = part & 3
        planes.append(part.astype(F32) - zeros)
    return jnp.concatenate(planes, axis=0)


def unpack_part(place, v_ref, o_ref, v_at, o_at, qv_ref, qo_ref):
    groups_v, groups_o = qv_ref.shape[1] // GROUP, qo_ref.shape[1] // GROUP
    cols_v = pl.ds(v_at, v_ref.shape[1])

    def v_group(group, carry):
        words = v_ref[pl.ds(pl.multiple_of(group * 8, 8), 8), :]
        zeros = v_ref[pl.ds(groups_v * 8 + group, 1), :].astype(F32)
        at = pl.ds(pl.multiple_of(group * GROUP, GROUP), GROUP)
        qv_ref[place, at, cols_v] = centred_planes(words, zeros).astype(BF16).astype(F8)
        return carry

    lax.fori_loop(0, groups_v, v_group, 0, unroll=4)

    def o_cols(block, carry):
        cols = pl.ds(pl.multiple_of(block * 512, 512), 512)
        cols_o = pl.ds(pl.multiple_of(o_at + block * 512, 512), 512)
        for group in range(groups_o):
            words = o_ref[group * 8:group * 8 + 8, cols]
            zeros = o_ref[groups_o * 8 + group:groups_o * 8 + group + 1, cols].astype(F32)
            at = slice(group * GROUP, (group + 1) * GROUP)
            qo_ref[place, at, cols_o] = centred_planes(words, zeros).astype(BF16).astype(F8)
        return carry

    lax.fori_loop(0, o_ref.shape[1] // 512, o_cols, 0)


def unpack_own_kernel(v_ref, o_ref, qv_ref, qo_ref):
    unpack_part(0, v_ref, o_ref, 0, 0, qv_ref, qo_ref)


def unpack_far_kernel(info_ref, v_same, v_other, o_same, o_other, own_sv, far_sv, own_so, far_so, qv_in, qo_in,
                      qv_ref, qo_ref, sv_ref, so_ref, gain_ref):
    core = info_ref[2]
    groups_o = so_ref.shape[1]
    for place, (sv, so) in enumerate(((own_sv, own_so), (far_sv, far_so))):
        sv_ref[place] = sv[...]
        so_ref[place] = so[:groups_o, :]
        gain_ref[place] = so[groups_o:, :]
    for v_ref, o_ref, half in ((v_same, o_same, core), (v_other, o_other, 1 - core)):
        v_at = pl.multiple_of(half * v_ref.shape[1], v_ref.shape[1])
        o_at = pl.multiple_of(half * o_ref.shape[1], o_ref.shape[1])
        unpack_part(1, v_ref, o_ref, v_at, o_at, qv_ref, qo_ref)


def turn_v_kernel(late, info_ref, unorder_ref, qv_ref, *rest):
    turned_ref = rest[-1]

    @pl.when((info_ref[0] >= LATE_STAGE) == late)
    def _():
        unorder = unorder_ref[...]
        for place in range(2):

            def group_turn(group, carry):
                at = pl.ds(pl.multiple_of(group * GROUP, GROUP), GROUP)
                turned_ref[place, :, at] = lax.dot_general(
                    qv_ref[place, at, :].astype(BF16), unorder, (((0,), (0,)), ((), ())),
                    preferred_element_type=F32).astype(F8)
                return carry

            lax.fori_loop(0, qv_ref.shape[1] // GROUP, group_turn, 0, unroll=8)


def turn_o_kernel(late, info_ref, unorder_ref, qo_ref, *rest):
    turned_ref = rest[-1]

    @pl.when((info_ref[0] >= LATE_STAGE) == late)
    def _():
        unorder = unorder_ref[...]
        for place in range(2):

            def cols_turn(block, carry):
                at = pl.ds(pl.multiple_of(block * 512, 512), 512)
                for group in range(qo_ref.shape[1] // GROUP):
                    span = slice(group * GROUP, (group + 1) * GROUP)
                    turned_ref[place, at, span] = lax.dot_general(
                        qo_ref[place, span, at].astype(BF16), unorder, (((0,), (0,)), ((), ())),
                        preferred_element_type=F32).astype(F8)
                return carry

            lax.fori_loop(0, qo_ref.shape[2] // 512, cols_turn, 0, unroll=2)


def split8(value):
    high = value.astype(F8).astype(F32)
    return high, (value - high) * 16.0


def merge8(out, start):
    return out[start:start + 16] + out[start + 16:start + 32] * 0.0625


def diag_pair(first, second):
    zero = jnp.zeros_like(first)
    return jnp.concatenate(
        [jnp.concatenate([first, zero], axis=1), jnp.concatenate([zero, second], axis=1)], axis=0
    )


def blocks_down(value):
    return jnp.concatenate([value[:, at:at + LANES] for at in range(0, value.shape[1], LANES)], axis=0)


def blocks_across(value, rows):
    return jnp.concatenate([value[at:at + rows] for at in range(0, value.shape[0], rows)], axis=1)


def row_inverse(states):
    return lax.rsqrt(jnp.mean(states * states, axis=-1, keepdims=True) + 1e-05)


def forward_layer(states, qv, qo, sv, so, gain_row, order, uv_ref, uo_ref, halfway):
    rows, width = states.shape
    normed = (states * row_inverse(states) * gain_row).astype(BF16)
    high, low = split8(jnp.dot(blocks_down(normed), order, preferred_element_type=F32))
    groups = width // GROUP
    tiles = jnp.concatenate(
        [high.reshape(groups, rows, LANES), low.reshape(groups, rows, LANES)], axis=1
    ).astype(F8)
    total = jnp.zeros((rows, sv.shape[1]), F32)
    for group in range(0, groups, 2):
        out = jnp.dot(
            diag_pair(tiles[group], tiles[group + 1]),
            qv[group * GROUP:(group + 2) * GROUP, :],
            preferred_element_type=F32,
        )
        for place in range(2):
            unit = merge8(out, 32 * place)
            uv_ref[group + place] = unit.astype(BF16)
            total = total + unit * sv[group + place:group + place + 1, :]
    halfway()
    values = total.astype(BF16)
    ordered = jnp.dot(blocks_down(values), order, preferred_element_type=F32)
    peak = jnp.maximum(jnp.max(jnp.abs(values.astype(F32)), axis=-1, keepdims=True), 1e-37)
    groups_o = values.shape[1] // GROUP
    tiles_o = []
    for group in range(groups_o):
        high, low = split8(ordered[group * rows:(group + 1) * rows] * (1.0 / peak) * F8_TOP)
        tiles_o.append(jnp.concatenate([high, low], axis=0).astype(F8))
    pairs = [diag_pair(tiles_o[group], tiles_o[group + 1]) for group in range(0, groups_o, 2)]
    back = peak * (1.0 / F8_TOP)
    updated = []
    for at in range(0, width, 512):
        moved = states[:, at:at + 512]
        for index, pair in enumerate(pairs):
            out = jnp.dot(pair, qo[index * 256:(index + 1) * 256, at:at + 512], preferred_element_type=F32)
            for place in range(2):
                group = 2 * index + place
                unit = merge8(out, 32 * place) * back
                uo_ref[group, :, at:at + 512] = unit.astype(BF16)
                moved = moved + unit * so[group:group + 1, at:at + 512]
        updated.append(moved.astype(BF16))
    return jnp.concatenate(updated, axis=1)


def forward_kernel(tick, micro, info_ref, arrived_ref, fresh_ref, qv_ref, qo_ref, sv_ref, so_ref, gain_ref, order_ref,
                   out_ref, states_hbm, uv_hbm, uo_hbm, states_ref, uv_ref, uo_ref, sems):
    z, swap = info_ref[0], info_ref[1]
    position = tick - SKEW * z

    def copies(index):
        return [
            pltpu.make_async_copy(here.at[index], there.at[index], sems.at[index, at])
            for at, (here, there) in enumerate(((states_ref, states_hbm), (uv_ref, uv_hbm), (uo_ref, uo_hbm)))
        ]

    def start(index, places):
        for copy in copies(index)[places]:
            copy.start()

    @pl.when((position >= 0) & (position < micro))
    def _():
        out_ref[...] = jnp.where(z == 0, fresh_ref[...], arrived_ref[...])
        order = order_ref[...]

        def layer(index, carry):
            place = index ^ swap
            states = out_ref[...]
            states_ref[index] = states
            out_ref[...] = forward_layer(
                states.astype(F32), qv_ref.at[place], qo_ref.at[place], sv_ref.at[place], so_ref.at[place],
                gain_ref[place], order, uv_ref.at[index], uo_ref.at[index], lambda: start(index, slice(0, 2)))
            start(index, slice(2, 3))
            return carry

        lax.fori_loop(0, 2, layer, 0)
        for index in range(2):
            for copy in copies(index):
                copy.wait()


def backward_layer(upstream, states, tv, to, sv, so, gain_row):
    rows, width = upstream.shape
    peak = jnp.maximum(jnp.max(jnp.abs(upstream), axis=-1, keepdims=True), 1e-37)
    scaled = upstream * (1.0 / peak) * (F8_TOP / STEP_O_MAX)
    groups_o = so.shape[0]
    found = []
    for group in range(0, groups_o, 2):
        parts = []
        for place in range(2):
            high, low = split8(scaled * so[group + place:group + place + 1, :])
            parts += [high, low]
        left = jnp.concatenate(parts, axis=0).astype(F8)
        out = jnp.dot(left, to[:, group * GROUP:(group + 2) * GROUP], preferred_element_type=F32)
        found += [merge8(out[:, :LANES], 0), merge8(out[:, LANES:], 32)]
    vgrad = (jnp.concatenate(found, axis=1) * (peak * (STEP_O_MAX / F8_TOP))).astype(BF16).astype(F32)
    peak = jnp.maximum(jnp.max(jnp.abs(vgrad), axis=-1, keepdims=True), 1e-37)
    scaled = vgrad * (1.0 / peak) * (F8_TOP / STEP_V_MAX)
    found = []
    for group in range(0, width // GROUP, 2):
        parts = []
        for place in range(2):
            high, low = split8(scaled * sv[group + place:group + place + 1, :])
            parts += [high, low]
        left = jnp.concatenate(parts, axis=0).astype(F8)
        out = jnp.dot(left, tv[:, group * GROUP:(group + 2) * GROUP], preferred_element_type=F32)
        found += [merge8(out[:, :LANES], 0), merge8(out[:, LANES:], 32)]
    ngrad = jnp.concatenate(found, axis=1) * gain_row * (peak * (STEP_V_MAX / F8_TOP))
    inverse = row_inverse(states)
    mixed = jnp.mean(ngrad * states, axis=-1, keepdims=True)
    moved = upstream + inverse * ngrad - states * (inverse * inverse * inverse) * mixed
    return moved.astype(BF16), vgrad.astype(BF16)


def backward_kernel(tick, micro, stages, places, info_ref, arrived_ref, fresh_ref, tv_ref, to_ref, sv_ref, so_ref, gain_ref,
                    *rest):
    stored, (out_ref, upstream_ref, vgrad_ref, states_ref, sem) = rest[:len(places)], rest[len(places):]
    z, swap = info_ref[0], info_ref[1]
    position = tick - SKEW * (stages - 1 - z)

    @pl.when((position >= 0) & (position < micro))
    def _():
        for place_at, source in zip(places, stored):

            @pl.when(z == place_at)
            def _():
                pltpu.make_async_copy(source, states_ref, sem).start()

        out_ref[...] = jnp.where(z == stages - 1, fresh_ref[...], arrived_ref[...])
        pltpu.make_async_copy(stored[0], states_ref, sem).wait()

        def layer(step, carry):
            index = 1 - step
            place = index ^ swap
            upstream = out_ref[...]
            upstream_ref[index] = upstream
            moved, vgrad = backward_layer(
                upstream.astype(F32), states_ref[index].astype(F32), tv_ref.at[place], to_ref.at[place],
                sv_ref.at[place], so_ref.at[place], gain_ref[place])
            out_ref[...] = moved
            vgrad_ref[index] = vgrad
            return carry

        lax.fori_loop(0, 2, layer, 0)


def grads_kernel(micro, stages, ticks, info_ref, *rest):
    kinds = [rest[kind * ticks:(kind + 1) * ticks] for kind in range(4)]
    gv_ref, go_ref, uv_ref, uo_ref, up_ref, vg_ref, sems = rest[4 * ticks:]
    targets = (uv_ref, uo_ref, up_ref, vg_ref)
    z = info_ref[0]
    for place in range(stages):

        @pl.when(z == place)
        def _():
            for index in range(2):
                for step in range(micro):
                    forth, back = SKEW * place + step, SKEW * (stages - 1 - place) + step
                    for kind, at in ((0, forth), (1, forth), (2, back), (3, back)):
                        pltpu.make_async_copy(
                            kinds[kind][at].at[index], targets[kind].at[index, step], sems.at[index, step, kind]).start()

    for index in range(2):
        for step in range(micro):
            for kind in range(4):
                pltpu.make_async_copy(
                    kinds[kind][0].at[index], targets[kind].at[index, step], sems.at[index, step, kind]).wait()
        vgrads = [vg_ref[index, step].astype(F32) for step in range(micro)]

        def groups_v(block, carry):
            sums = []
            for at in range(8):
                total = uv_ref[index, 0, block * 8 + at].astype(F32) * vgrads[0]
                for step in range(1, micro):
                    total = total + uv_ref[index, step, block * 8 + at].astype(F32) * vgrads[step]
                sums.append(jnp.sum(total, axis=0, keepdims=True))
            gv_ref[index, pl.ds(pl.multiple_of(block * 8, 8), 8), :] = jnp.concatenate(sums, axis=0)
            return carry

        lax.fori_loop(0, gv_ref.shape[1] // 8, groups_v, 0)

        def cols_o(block, carry):
            cols = pl.ds(pl.multiple_of(block * 512, 512), 512)
            ups = [up_ref[index, step, :, cols].astype(F32) for step in range(micro)]
            sums = []
            for group in range(go_ref.shape[1]):
                total = uo_ref[index, 0, group, :, cols].astype(F32) * ups[0]
                for step in range(1, micro):
                    total = total + uo_ref[index, step, group, :, cols].astype(F32) * ups[step]
                sums.append(jnp.sum(total, axis=0, keepdims=True))
            go_ref[index, :, cols] = jnp.concatenate(sums, axis=0)
            return carry

        lax.fori_loop(0, go_ref.shape[2] // 512, cols_o, 0)


VMEM = pl.BlockSpec(memory_space=pltpu.VMEM)
SMEM = pl.BlockSpec(memory_space=pltpu.SMEM)
HBM = pl.BlockSpec(memory_space=pltpu.HBM)


def on_chip(value):
    return pltpu.with_memory_space_constraint(value, pltpu.VMEM)


def in_hbm(values):
    return [pltpu.with_memory_space_constraint(value, pltpu.HBM) for value in values]


def kernel_call(body, outs, in_specs, out_specs, scratch=(), aliases=None, flops=0, moved=0, name=None, vmem=VMEM_BYTES):
    return pl.pallas_call(
        body,
        out_shape=outs,
        in_specs=in_specs,
        out_specs=out_specs,
        scratch_shapes=list(scratch),
        input_output_aliases=aliases or {},
        compiler_params=pltpu.CompilerParams(vmem_limit_bytes=vmem),
        cost_estimate=pl.CostEstimate(flops=flops, bytes_accessed=moved, transcendentals=0),
        name=name,
    )


def fixed_swap(value, axis, bit):
    count = lax.axis_size(axis)
    return lax.ppermute(value, axis, [(source, source ^ bit) for source in range(count)])


def half_codes(words, core):
    low, high = jnp.split(words, 2, axis=1)
    return fixed_swap(jnp.where(core == 0, low, high), "section", 1)


def ends_rows(hidden_in, cotangent, stages):
    micro, rows, part = hidden_in.shape
    half = micro // 2
    hidden = hidden_in.reshape(2, half, rows, part).transpose(1, 0, 2, 3)
    last = cotangent.reshape(2, half, rows, part).transpose(1, 0, 2, 3)
    pieces = jnp.concatenate([hidden, last[::-1]]).reshape(4 * half, rows, part)
    found = lax.all_to_all(pieces, "section", 0, 0)
    found = found.transpose(1, 0, 2).reshape(rows, 4 * half * part)
    routes = []
    for place in range(1, half):
        for side_at in range(2):
            routes.append((2 * place + side_at, 2 * (place - 1) + side_at))
            routes.append((2 * (stages - 1 - place) + side_at, 2 * (stages - place) + side_at))
    ends = [found]
    for _ in range(half - 1):
        ends.append(lax.ppermute(ends[-1], "section", routes))
    return ends


def gather_steps(value):
    count = lax.axis_size("dp")
    return lax.all_to_all(jnp.broadcast_to(value[None], (count,) + value.shape), "dp", 0, 0)


def scatter_sums(value, side):
    mine = jnp.where(side == 0, value[0], value[1])
    other = jnp.where(side == 0, value[1], value[0])
    total = mine + fixed_swap(other.astype(BF16), "section", 1).astype(F32)
    return jnp.sum(lax.all_to_all(total.astype(BF16), "dp", 0, 0).astype(F32), axis=0)


def on_device(hidden_in, cotangent, codes_v, zeros_v, steps_v, codes_o, zeros_o, steps_o, gain):
    section_id = lax.axis_index("section")
    section_count = lax.axis_size("section")
    dp_count = lax.axis_size("dp")
    z, side = section_id // 2, section_id % 2
    stages = section_count // 2
    micro = hidden_in.shape[0] // 2
    rows = hidden_in.shape[1]
    width, value_width = gain.shape[1], codes_v.shape[2]
    groups_v, groups_o = zeros_v.shape[1], zeros_o.shape[1]

    own_v = jnp.concatenate([pair_words(codes_v[0]), zeros_v[0]], axis=0)
    own_o = jnp.concatenate([pair_words(codes_o[0]), zeros_o[0]], axis=0)
    core = lax.axis_index("dp") % 2
    same_v, same_o = half_codes(own_v, core), half_codes(own_o, core)
    ends = ends_rows(hidden_in, cotangent, stages)
    count_v, count_o = steps_v.size, steps_o.size
    steps = gather_steps(jnp.concatenate([steps_v.reshape(-1), steps_o.reshape(-1)]))
    own_sv = steps[:, :count_v].reshape(dp_count, groups_v, -1).transpose(1, 0, 2).reshape(groups_v, value_width)
    own_so = steps[:, count_v:].reshape(dp_count, groups_o, -1).transpose(1, 0, 2).reshape(groups_o, width)
    own_so = jnp.concatenate([own_so, gain], axis=0)
    other_v, other_o = fixed_swap(same_v, "dp", 1), fixed_swap(same_o, "dp", 1)
    far_sv, far_so = fixed_swap(own_sv, "section", 1), fixed_swap(own_so, "section", 1)
    order, unorder = order_matrices()
    info = jnp.stack([z, side, core]).astype(I32)
    own_v, own_o, own_sv, own_so, order, unorder, info, ends[0] = lax.optimization_barrier(
        (own_v, own_o, own_sv, own_so, order, unorder, info, ends[0]))

    q_shapes = (pltpu.VMEM((2, width, value_width), F8), pltpu.VMEM((2, value_width, width), F8))
    qv, qo = kernel_call(
        unpack_own_kernel, q_shapes, [VMEM] * 2, (VMEM, VMEM), flops=10**8, moved=2**22, name="unpack_own",
    )(own_v, own_o)
    qv, qo, sv, so, gains = kernel_call(
        unpack_far_kernel,
        q_shapes + tuple(jax.ShapeDtypeStruct(shape, F32) for shape in (
            (2, groups_v, value_width), (2, groups_o, width), (2, 1, width))),
        [SMEM] + [VMEM] * 10, (VMEM,) * 5, aliases={9: 0, 10: 1}, flops=10**8, moved=2**22, name="unpack_far",
    )(info, same_v, other_v, same_o, other_o, own_sv, far_sv, own_so, far_so, on_chip(qv), on_chip(qo))
    qv, qo = on_chip(qv), on_chip(qo)

    t_shapes = (pltpu.VMEM((2, value_width, width), F8), pltpu.VMEM((2, width, value_width), F8))
    turned = [None, None]

    def turn(which, late, unorder):
        body = (turn_v_kernel, turn_o_kernel)[which]
        known = [] if turned[which] is None else [on_chip(turned[which])]
        turned[which] = kernel_call(
            lambda *refs: body(late, *refs), t_shapes[which], [SMEM] + [VMEM] * (2 + len(known)), VMEM,
            aliases={3: 0} if known else {}, flops=10**8, moved=2**22, name="turn",
        )(info, unorder, (qv, qo)[which], *known)

    uv_shape, uo_shape = (2, groups_v, rows, value_width), (2, groups_o, rows, width)
    stored_shapes = [(2, rows, width), uv_shape, uo_shape]
    flops = 4 * 2 * rows * width * value_width * 2
    last = stages - 1
    ticks = micro + SKEW * last

    def forward(tick, arrived):
        done = kernel_call(
            lambda *refs: forward_kernel(tick, micro, *refs),
            (jax.ShapeDtypeStruct((rows, width), BF16),) + tuple(pltpu.HBM(shape, BF16) for shape in stored_shapes),
            [SMEM] + [VMEM] * 8, (VMEM, HBM, HBM, HBM),
            scratch=[pltpu.VMEM(shape, BF16) for shape in stored_shapes] + [pltpu.SemaphoreType.DMA((2, 3))],
            flops=flops, moved=2**24, name="forward",
        )(info, arrived, ends[min(tick, micro - 1)], qv, qo, sv, so, gains, order)
        return done[0], done[1:]

    def backward(tick, arrived, stored):
        places = [place for place in range(stages) if 0 <= tick - SKEW * (last - place) < micro]
        sources = [stored[SKEW * place + tick - SKEW * (last - place)][0] for place in places]
        return kernel_call(
            lambda *refs: backward_kernel(tick, micro, stages, places, *refs),
            (jax.ShapeDtypeStruct((rows, width), BF16), pltpu.HBM((2, rows, width), BF16),
             pltpu.HBM((2, rows, value_width), BF16)),
            [SMEM] + [VMEM] * 7 + [HBM] * len(places), (VMEM,) * 3,
            scratch=[pltpu.VMEM((2, rows, width), BF16), pltpu.SemaphoreType.DMA], flops=flops, moved=2**24, name="backward",
        )(info, arrived, ends[min(tick, micro - 1)], on_chip(turned[0]), on_chip(turned[1]), sv, so, gains, *in_hbm(sources))

    up_routes = [(source, source + 2) for source in range(section_count - 2)]
    down_routes = [(source + 2, source) for source in range(section_count - 2)]
    empty = jnp.zeros((rows, width), BF16)
    sent_f, sent_b, stored, backs = [], [], [], []
    for tick in range(2 * ticks - micro + 1):
        if tick < ticks:
            out, kept = forward(tick, sent_f[tick - SKEW] if tick >= SKEW else empty)
            stored.append(kept)
            sent_f.append(lax.ppermute(out, "section", up_routes) if tick < ticks - SKEW else None)
            for first, late in ((1, True), (ticks - 6, False)):
                which = tick - first
                if 0 <= which < 2:
                    turn(which, late, lax.optimization_barrier((unorder, out))[0])
                    if tick + 1 >= SKEW:
                        at = tick + 1 - SKEW
                        sent_f[at], turned[which] = lax.optimization_barrier((sent_f[at], turned[which]))
        back = tick - (ticks - micro + 1)
        if back >= 0:
            out, upstream, vgrad = backward(back, sent_b[back - SKEW] if back >= SKEW else empty, stored)
            backs.append((upstream, vgrad))
            sent_b.append(lax.ppermute(out, "section", down_routes) if back < ticks - SKEW else None)

    stored_all = [kept[1] for kept in stored] + [kept[2] for kept in stored]
    stored_all += [back[0] for back in backs] + [back[1] for back in backs]
    sums = kernel_call(
        lambda *refs: grads_kernel(micro, stages, ticks, *refs),
        (jax.ShapeDtypeStruct((2, groups_v, value_width), F32), jax.ShapeDtypeStruct((2, groups_o, width), F32)),
        [SMEM] + [HBM] * len(stored_all), (VMEM, VMEM),
        scratch=[pltpu.VMEM((2, micro) + shape, BF16) for shape in (uv_shape[1:], uo_shape[1:], (rows, width), (rows, value_width))]
        + [pltpu.SemaphoreType.DMA((2, micro, 4))],
        flops=10**7, moved=2**24, name="grads", vmem=32 * 2**20,
    )(info, *in_hbm(stored_all))

    total_v = sums[0].reshape(2, groups_v, dp_count, -1).transpose(0, 2, 1, 3).reshape(2, dp_count, -1)
    total_o = sums[1].reshape(2, groups_o, dp_count, -1).transpose(0, 2, 1, 3).reshape(2, dp_count, -1)
    total = scatter_sums(jnp.concatenate([total_v, total_o], axis=2), side)
    return total[:count_v].reshape(steps_v.shape), total[count_v:].reshape(steps_o.shape)


def solution(mesh):
    return jax.shard_map(
        on_device,
        mesh=mesh,
        in_specs=(
            P(None, "dp", "section"),
            P(None, "dp", "section"),
            P("section", None, None),
            P("section", None, None),
            P("section", None, "dp"),
            P("section", None, None),
            P("section", None, None),
            P("section", None, "dp"),
            P("section", None),
        ),
        out_specs=(P("section", None, "dp"), P("section", None, "dp")),
        check_vma=False,
    )
```

```python
import jax
import jax.numpy as jnp
from jax import lax
from jax.experimental import pallas as pl
from jax.experimental.pallas import tpu as pltpu
from jax.sharding import PartitionSpec as P

F32, BF16, I32, F8 = jnp.float32, jnp.bfloat16, jnp.int32, jnp.float8_e4m3fn
GROUP = 128
LANES = 128
VMEM_BYTES = 12 * 2**20
STEP_V_MAX = 0.0144
STEP_O_MAX = 0.0575
F8_TOP = 400.0
SKEW = 2
LATE_STAGE = 4


def pair_words(words):
    rows, cols = words.shape
    shaped = words.reshape(rows // 16, 2, 8, cols)
    return (shaped[:, 0] | (shaped[:, 1] << 16)).reshape(rows // 2, cols)


def order_matrices():
    place = jnp.arange(LANES, dtype=I32)
    field, row = place // 8, place % 8
    natural = jnp.where(field < 8, 8 * row + field, 64 + 8 * row + field - 8)
    gather = (jnp.arange(LANES, dtype=I32)[:, None] == natural[None, :]).astype(BF16)
    return gather, gather.T


def centred_planes(words, zeros):
    planes = []
    for field in range(16):
        part = lax.shift_right_logical(words, jnp.int32(2 * field))
        if field < 15:
            part = part & 3
        planes.append(part.astype(F32) - zeros)
    return jnp.concatenate(planes, axis=0)


def unpack_part(place, v_ref, o_ref, v_at, o_at, qv_ref, qo_ref):
    groups_v, groups_o = qv_ref.shape[1] // GROUP, qo_ref.shape[1] // GROUP
    cols_v = pl.ds(v_at, v_ref.shape[1])

    def v_group(group, carry):
        words = v_ref[pl.ds(pl.multiple_of(group * 8, 8), 8), :]
        zeros = v_ref[pl.ds(groups_v * 8 + group, 1), :].astype(F32)
        at = pl.ds(pl.multiple_of(group * GROUP, GROUP), GROUP)
        qv_ref[place, at, cols_v] = centred_planes(words, zeros).astype(BF16).astype(F8)
        return carry

    lax.fori_loop(0, groups_v, v_group, 0, unroll=4)

    def o_cols(block, carry):
        cols = pl.ds(pl.multiple_of(block * 512, 512), 512)
        cols_o = pl.ds(pl.multiple_of(o_at + block * 512, 512), 512)
        for group in range(groups_o):
            words = o_ref[group * 8:group * 8 + 8, cols]
            zeros = o_ref[groups_o * 8 + group:groups_o * 8 + group + 1, cols].astype(F32)
            at = slice(group * GROUP, (group + 1) * GROUP)
            qo_ref[place, at, cols_o] = centred_planes(words, zeros).astype(BF16).astype(F8)
        return carry

    lax.fori_loop(0, o_ref.shape[1] // 512, o_cols, 0)


def unpack_own_kernel(v_ref, o_ref, qv_ref, qo_ref):
    unpack_part(0, v_ref, o_ref, 0, 0, qv_ref, qo_ref)


def unpack_far_kernel(info_ref, v_same, v_other, o_same, o_other, own_sv, far_sv, own_so, far_so, qv_in, qo_in,
                      qv_ref, qo_ref, sv_ref, so_ref, gain_ref):
    core = info_ref[2]
    groups_o = so_ref.shape[1]
    for place, (sv, so) in enumerate(((own_sv, own_so), (far_sv, far_so))):
        sv_ref[place] = sv[...]
        so_ref[place] = so[:groups_o, :]
        gain_ref[place] = so[groups_o:, :]
    for v_ref, o_ref, half in ((v_same, o_same, core), (v_other, o_other, 1 - core)):
        v_at = pl.multiple_of(half * v_ref.shape[1], v_ref.shape[1])
        o_at = pl.multiple_of(half * o_ref.shape[1], o_ref.shape[1])
        unpack_part(1, v_ref, o_ref, v_at, o_at, qv_ref, qo_ref)


def turn_v_kernel(late, info_ref, unorder_ref, qv_ref, *rest):
    turned_ref = rest[-1]

    @pl.when((info_ref[0] >= LATE_STAGE) == late)
    def _():
        unorder = unorder_ref[...]
        for place in range(2):

            def group_turn(group, carry):
                at = pl.ds(pl.multiple_of(group * GROUP, GROUP), GROUP)
                turned_ref[place, :, at] = lax.dot_general(
                    qv_ref[place, at, :].astype(BF16), unorder, (((0,), (0,)), ((), ())),
                    preferred_element_type=F32).astype(F8)
                return carry

            lax.fori_loop(0, qv_ref.shape[1] // GROUP, group_turn, 0, unroll=8)


def turn_o_kernel(late, info_ref, unorder_ref, qo_ref, *rest):
    turned_ref = rest[-1]

    @pl.when((info_ref[0] >= LATE_STAGE) == late)
    def _():
        unorder = unorder_ref[...]
        for place in range(2):

            def cols_turn(block, carry):
                at = pl.ds(pl.multiple_of(block * 512, 512), 512)
                for group in range(qo_ref.shape[1] // GROUP):
                    span = slice(group * GROUP, (group + 1) * GROUP)
                    turned_ref[place, at, span] = lax.dot_general(
                        qo_ref[place, span, at].astype(BF16), unorder, (((0,), (0,)), ((), ())),
                        preferred_element_type=F32).astype(F8)
                return carry

            lax.fori_loop(0, qo_ref.shape[2] // 512, cols_turn, 0, unroll=2)


def split8(value):
    high = value.astype(F8).astype(F32)
    return high, (value - high) * 16.0


def merge8(out, start):
    return out[start:start + 16] + out[start + 16:start + 32] * 0.0625


def diag_pair(first, second):
    zero = jnp.zeros_like(first)
    return jnp.concatenate(
        [jnp.concatenate([first, zero], axis=1), jnp.concatenate([zero, second], axis=1)], axis=0
    )


def blocks_down(value):
    return jnp.concatenate([value[:, at:at + LANES] for at in range(0, value.shape[1], LANES)], axis=0)


def blocks_across(value, rows):
    return jnp.concatenate([value[at:at + rows] for at in range(0, value.shape[0], rows)], axis=1)


def row_inverse(states):
    return lax.rsqrt(jnp.mean(states * states, axis=-1, keepdims=True) + 1e-05)


def forward_layer(states, qv, qo, sv, so, gain_row, order, uv_ref, uo_ref, halfway):
    rows, width = states.shape
    normed = (states * row_inverse(states) * gain_row).astype(BF16)
    high, low = split8(jnp.dot(blocks_down(normed), order, preferred_element_type=F32))
    groups = width // GROUP
    tiles = jnp.concatenate(
        [high.reshape(groups, rows, LANES), low.reshape(groups, rows, LANES)], axis=1
    ).astype(F8)
    total = jnp.zeros((rows, sv.shape[1]), F32)
    for group in range(0, groups, 2):
        out = jnp.dot(
            diag_pair(tiles[group], tiles[group + 1]),
            qv[group * GROUP:(group + 2) * GROUP, :],
            preferred_element_type=F32,
        )
        for place in range(2):
            unit = merge8(out, 32 * place)
            uv_ref[group + place] = unit.astype(BF16)
            total = total + unit * sv[group + place:group + place + 1, :]
    halfway()
    values = total.astype(BF16)
    ordered = jnp.dot(blocks_down(values), order, preferred_element_type=F32)
    peak = jnp.maximum(jnp.max(jnp.abs(values.astype(F32)), axis=-1, keepdims=True), 1e-37)
    groups_o = values.shape[1] // GROUP
    tiles_o = []
    for group in range(groups_o):
        high, low = split8(ordered[group * rows:(group + 1) * rows] * (1.0 / peak) * F8_TOP)
        tiles_o.append(jnp.concatenate([high, low], axis=0).astype(F8))
    pairs = [diag_pair(tiles_o[group], tiles_o[group + 1]) for group in range(0, groups_o, 2)]
    back = peak * (1.0 / F8_TOP)
    updated = []
    for at in range(0, width, 512):
        moved = states[:, at:at + 512]
        for index, pair in enumerate(pairs):
            out = jnp.dot(pair, qo[index * 256:(index + 1) * 256, at:at + 512], preferred_element_type=F32)
            for place in range(2):
                group = 2 * index + place
                unit = merge8(out, 32 * place) * back
                uo_ref[group, :, at:at + 512] = unit.astype(BF16)
                moved = moved + unit * so[group:group + 1, at:at + 512]
        updated.append(moved.astype(BF16))
    return jnp.concatenate(updated, axis=1)


def forward_kernel(tick, micro, info_ref, arrived_ref, fresh_ref, qv_ref, qo_ref, sv_ref, so_ref, gain_ref, order_ref,
                   out_ref, states_hbm, uv_hbm, uo_hbm, states_ref, uv_ref, uo_ref, sems):
    z, swap = info_ref[0], info_ref[1]
    position = tick - SKEW * z

    def copies(index):
        return [
            pltpu.make_async_copy(here.at[index], there.at[index], sems.at[index, at])
            for at, (here, there) in enumerate(((states_ref, states_hbm), (uv_ref, uv_hbm), (uo_ref, uo_hbm)))
        ]

    def start(index, places):
        for copy in copies(index)[places]:
            copy.start()

    @pl.when((position >= 0) & (position < micro))
    def _():
        out_ref[...] = jnp.where(z == 0, fresh_ref[...], arrived_ref[...])
        order = order_ref[...]

        def layer(index, carry):
            place = index ^ swap
            states = out_ref[...]
            states_ref[index] = states
            out_ref[...] = forward_layer(
                states.astype(F32), qv_ref.at[place], qo_ref.at[place], sv_ref.at[place], so_ref.at[place],
                gain_ref[place], order, uv_ref.at[index], uo_ref.at[index], lambda: start(index, slice(0, 2)))
            start(index, slice(2, 3))
            return carry

        lax.fori_loop(0, 2, layer, 0)
        for index in range(2):
            for copy in copies(index):
                copy.wait()


def backward_layer(upstream, states, tv, to, sv, so, gain_row):
    rows, width = upstream.shape
    peak = jnp.maximum(jnp.max(jnp.abs(upstream), axis=-1, keepdims=True), 1e-37)
    scaled = upstream * (1.0 / peak) * (F8_TOP / STEP_O_MAX)
    groups_o = so.shape[0]
    found = []
    for group in range(0, groups_o, 2):
        parts = []
        for place in range(2):
            high, low = split8(scaled * so[group + place:group + place + 1, :])
            parts += [high, low]
        left = jnp.concatenate(parts, axis=0).astype(F8)
        out = jnp.dot(left, to[:, group * GROUP:(group + 2) * GROUP], preferred_element_type=F32)
        found += [merge8(out[:, :LANES], 0), merge8(out[:, LANES:], 32)]
    vgrad = (jnp.concatenate(found, axis=1) * (peak * (STEP_O_MAX / F8_TOP))).astype(BF16).astype(F32)
    peak = jnp.maximum(jnp.max(jnp.abs(vgrad), axis=-1, keepdims=True), 1e-37)
    scaled = vgrad * (1.0 / peak) * (F8_TOP / STEP_V_MAX)
    found = []
    for group in range(0, width // GROUP, 2):
        parts = []
        for place in range(2):
            high, low = split8(scaled * sv[group + place:group + place + 1, :])
            parts += [high, low]
        left = jnp.concatenate(parts, axis=0).astype(F8)
        out = jnp.dot(left, tv[:, group * GROUP:(group + 2) * GROUP], preferred_element_type=F32)
        found += [merge8(out[:, :LANES], 0), merge8(out[:, LANES:], 32)]
    ngrad = jnp.concatenate(found, axis=1) * gain_row * (peak * (STEP_V_MAX / F8_TOP))
    inverse = row_inverse(states)
    mixed = jnp.mean(ngrad * states, axis=-1, keepdims=True)
    moved = upstream + inverse * ngrad - states * (inverse * inverse * inverse) * mixed
    return moved.astype(BF16), vgrad.astype(BF16)


def backward_kernel(tick, micro, stages, places, info_ref, arrived_ref, fresh_ref, tv_ref, to_ref, sv_ref, so_ref, gain_ref,
                    *rest):
    stored = rest[:len(places)]
    out_ref, upstream_hbm, vgrad_hbm, states_ref, upstream_ref, vgrad_ref, sem, sems = rest[len(places):]
    z, swap = info_ref[0], info_ref[1]
    position = tick - SKEW * (stages - 1 - z)

    def upstream_copy(index):
        return pltpu.make_async_copy(upstream_ref.at[index], upstream_hbm.at[index], sems.at[index, 0])

    def vgrad_copy(index):
        return pltpu.make_async_copy(vgrad_ref.at[index], vgrad_hbm.at[index], sems.at[index, 1])

    @pl.when((position >= 0) & (position < micro))
    def _():
        for place_at, source in zip(places, stored):

            @pl.when(z == place_at)
            def _():
                pltpu.make_async_copy(source, states_ref, sem).start()

        out_ref[...] = jnp.where(z == stages - 1, fresh_ref[...], arrived_ref[...])
        pltpu.make_async_copy(stored[0], states_ref, sem).wait()

        def layer(step, carry):
            index = 1 - step
            place = index ^ swap
            upstream = out_ref[...]
            upstream_ref[index] = upstream
            upstream_copy(index).start()
            moved, vgrad = backward_layer(
                upstream.astype(F32), states_ref[index].astype(F32), tv_ref.at[place], to_ref.at[place],
                sv_ref.at[place], so_ref.at[place], gain_ref[place])
            out_ref[...] = moved
            vgrad_ref[index] = vgrad
            vgrad_copy(index).start()
            return carry

        lax.fori_loop(0, 2, layer, 0)
        for index in range(2):
            upstream_copy(index).wait()
            vgrad_copy(index).wait()


def grads_kernel(micro, stages, ticks, info_ref, *rest):
    kinds = [rest[kind * ticks:(kind + 1) * ticks] for kind in range(4)]
    gv_ref, go_ref, uv_ref, uo_ref, up_ref, vg_ref, sems = rest[4 * ticks:]
    targets = (uv_ref, uo_ref, up_ref, vg_ref)
    z = info_ref[0]
    for place in range(stages):

        @pl.when(z == place)
        def _():
            for index in range(2):
                for kind, step in [(kind, step) for kind in (3, 0, 2, 1) for step in range(micro)]:
                    at = step + SKEW * (place if kind < 2 else stages - 1 - place)
                    pltpu.make_async_copy(
                        kinds[kind][at].at[index], targets[kind].at[index, step], sems.at[index, step, kind]).start()

    def arrive(index, chosen):
        for step in range(micro):
            for kind in chosen:
                pltpu.make_async_copy(
                    kinds[kind][0].at[index], targets[kind].at[index, step], sems.at[index, step, kind]).wait()

    for index in range(2):
        arrive(index, (0, 3))
        vgrads = [vg_ref[index, step].astype(F32) for step in range(micro)]

        def groups_v(block, carry):
            sums = []
            for at in range(8):
                total = uv_ref[index, 0, block * 8 + at].astype(F32) * vgrads[0]
                for step in range(1, micro):
                    total = total + uv_ref[index, step, block * 8 + at].astype(F32) * vgrads[step]
                sums.append(jnp.sum(total, axis=0, keepdims=True))
            gv_ref[index, pl.ds(pl.multiple_of(block * 8, 8), 8), :] = jnp.concatenate(sums, axis=0)
            return carry

        lax.fori_loop(0, gv_ref.shape[1] // 8, groups_v, 0)

        arrive(index, (1, 2))

        def cols_o(block, carry):
            cols = pl.ds(pl.multiple_of(block * 512, 512), 512)
            ups = [up_ref[index, step, :, cols].astype(F32) for step in range(micro)]
            sums = []
            for group in range(go_ref.shape[1]):
                total = uo_ref[index, 0, group, :, cols].astype(F32) * ups[0]
                for step in range(1, micro):
                    total = total + uo_ref[index, step, group, :, cols].astype(F32) * ups[step]
                sums.append(jnp.sum(total, axis=0, keepdims=True))
            go_ref[index, :, cols] = jnp.concatenate(sums, axis=0)
            return carry

        lax.fori_loop(0, go_ref.shape[2] // 512, cols_o, 0)


VMEM = pl.BlockSpec(memory_space=pltpu.VMEM)
SMEM = pl.BlockSpec(memory_space=pltpu.SMEM)
HBM = pl.BlockSpec(memory_space=pltpu.HBM)


def on_chip(value):
    return pltpu.with_memory_space_constraint(value, pltpu.VMEM)


def in_hbm(values):
    return [pltpu.with_memory_space_constraint(value, pltpu.HBM) for value in values]


def kernel_call(body, outs, in_specs, out_specs, scratch=(), aliases=None, flops=0, moved=0, name=None, vmem=VMEM_BYTES):
    return pl.pallas_call(
        body,
        out_shape=outs,
        in_specs=in_specs,
        out_specs=out_specs,
        scratch_shapes=list(scratch),
        input_output_aliases=aliases or {},
        compiler_params=pltpu.CompilerParams(vmem_limit_bytes=vmem),
        cost_estimate=pl.CostEstimate(flops=flops, bytes_accessed=moved, transcendentals=0),
        name=name,
    )


def fixed_swap(value, axis, bit):
    count = lax.axis_size(axis)
    return lax.ppermute(value, axis, [(source, source ^ bit) for source in range(count)])


def half_codes(words, core):
    low, high = jnp.split(words, 2, axis=1)
    return fixed_swap(jnp.where(core == 0, low, high), "section", 1)


def ends_rows(hidden_in, cotangent, stages):
    micro, rows, part = hidden_in.shape
    half = micro // 2
    hidden = hidden_in.reshape(2, half, rows, part).transpose(1, 0, 2, 3)
    last = cotangent.reshape(2, half, rows, part).transpose(1, 0, 2, 3)
    pieces = jnp.concatenate([hidden, last[::-1]]).reshape(4 * half, rows, part)
    found = lax.all_to_all(pieces, "section", 0, 0)
    found = found.transpose(1, 0, 2).reshape(rows, 4 * half * part)
    routes = []
    for place in range(1, half):
        for side_at in range(2):
            routes.append((2 * place + side_at, 2 * (place - 1) + side_at))
            routes.append((2 * (stages - 1 - place) + side_at, 2 * (stages - place) + side_at))
    ends = [found]
    for _ in range(half - 1):
        ends.append(lax.ppermute(ends[-1], "section", routes))
    return ends


def gather_steps(value):
    count = lax.axis_size("dp")
    return lax.all_to_all(jnp.broadcast_to(value[None], (count,) + value.shape), "dp", 0, 0)


def scatter_sums(value, side):
    mine = jnp.where(side == 0, value[0], value[1])
    other = jnp.where(side == 0, value[1], value[0])
    total = mine + fixed_swap(other.astype(BF16), "section", 1).astype(F32)
    return jnp.sum(lax.all_to_all(total.astype(BF16), "dp", 0, 0).astype(F32), axis=0)


def on_device(hidden_in, cotangent, codes_v, zeros_v, steps_v, codes_o, zeros_o, steps_o, gain):
    section_id = lax.axis_index("section")
    section_count = lax.axis_size("section")
    dp_count = lax.axis_size("dp")
    z, side = section_id // 2, section_id % 2
    stages = section_count // 2
    micro = hidden_in.shape[0] // 2
    rows = hidden_in.shape[1]
    width, value_width = gain.shape[1], codes_v.shape[2]
    groups_v, groups_o = zeros_v.shape[1], zeros_o.shape[1]

    own_v = jnp.concatenate([pair_words(codes_v[0]), zeros_v[0]], axis=0)
    own_o = jnp.concatenate([pair_words(codes_o[0]), zeros_o[0]], axis=0)
    core = lax.axis_index("dp") % 2
    same_v, same_o = half_codes(own_v, core), half_codes(own_o, core)
    ends = ends_rows(hidden_in, cotangent, stages)
    count_v, count_o = steps_v.size, steps_o.size
    steps = gather_steps(jnp.concatenate([steps_v.reshape(-1), steps_o.reshape(-1)]).astype(BF16)).astype(F32)
    own_sv = steps[:, :count_v].reshape(dp_count, groups_v, -1).transpose(1, 0, 2).reshape(groups_v, value_width)
    own_so = steps[:, count_v:].reshape(dp_count, groups_o, -1).transpose(1, 0, 2).reshape(groups_o, width)
    own_so = jnp.concatenate([own_so, gain], axis=0)
    far_sv, far_so = fixed_swap(own_sv, "section", 1), fixed_swap(own_so, "section", 1)
    order, unorder = order_matrices()
    info = jnp.stack([z, side, core]).astype(I32)
    own_v, own_o, own_sv, own_so, same_v, same_o, order, unorder, info, ends[0] = lax.optimization_barrier(
        (own_v, own_o, own_sv, own_so, same_v, same_o, order, unorder, info, ends[0]))
    other_v, other_o = fixed_swap(same_v, "dp", 1), fixed_swap(same_o, "dp", 1)

    q_shapes = (pltpu.VMEM((2, width, value_width), F8), pltpu.VMEM((2, value_width, width), F8))
    qv, qo = kernel_call(
        unpack_own_kernel, q_shapes, [VMEM] * 2, (VMEM, VMEM), flops=10**8, moved=2**22, name="unpack_own",
    )(own_v, own_o)
    qv, qo, sv, so, gains = kernel_call(
        unpack_far_kernel,
        q_shapes + tuple(jax.ShapeDtypeStruct(shape, F32) for shape in (
            (2, groups_v, value_width), (2, groups_o, width), (2, 1, width))),
        [SMEM] + [VMEM] * 10, (VMEM,) * 5, aliases={9: 0, 10: 1}, flops=10**8, moved=2**22, name="unpack_far",
    )(info, same_v, other_v, same_o, other_o, own_sv, far_sv, own_so, far_so, on_chip(qv), on_chip(qo))
    qv, qo = on_chip(qv), on_chip(qo)

    t_shapes = (pltpu.VMEM((2, value_width, width), F8), pltpu.VMEM((2, width, value_width), F8))
    turned = [None, None]

    def turn(which, late, unorder):
        body = (turn_v_kernel, turn_o_kernel)[which]
        known = [] if turned[which] is None else [on_chip(turned[which])]
        turned[which] = kernel_call(
            lambda *refs: body(late, *refs), t_shapes[which], [SMEM] + [VMEM] * (2 + len(known)), VMEM,
            aliases={3: 0} if known else {}, flops=10**8, moved=2**22, name="turn",
        )(info, unorder, (qv, qo)[which], *known)

    uv_shape, uo_shape = (2, groups_v, rows, value_width), (2, groups_o, rows, width)
    stored_shapes = [(2, rows, width), uv_shape, uo_shape]
    flops = 4 * 2 * rows * width * value_width * 2
    last = stages - 1
    ticks = micro + SKEW * last

    def forward(tick, arrived):
        done = kernel_call(
            lambda *refs: forward_kernel(tick, micro, *refs),
            (jax.ShapeDtypeStruct((rows, width), BF16),) + tuple(pltpu.HBM(shape, BF16) for shape in stored_shapes),
            [SMEM] + [VMEM] * 8, (VMEM, HBM, HBM, HBM),
            scratch=[pltpu.VMEM(shape, BF16) for shape in stored_shapes] + [pltpu.SemaphoreType.DMA((2, 3))],
            flops=flops, moved=2**24, name="forward",
        )(info, arrived, ends[min(tick, micro - 1)], qv, qo, sv, so, gains, order)
        return done[0], done[1:]

    def backward(tick, arrived, stored):
        places = [place for place in range(stages) if 0 <= tick - SKEW * (last - place) < micro]
        sources = [stored[SKEW * place + tick - SKEW * (last - place)][0] for place in places]
        return kernel_call(
            lambda *refs: backward_kernel(tick, micro, stages, places, *refs),
            (jax.ShapeDtypeStruct((rows, width), BF16), pltpu.HBM((2, rows, width), BF16),
             pltpu.HBM((2, rows, value_width), BF16)),
            [SMEM] + [VMEM] * 7 + [HBM] * len(places), (VMEM, HBM, HBM),
            scratch=[pltpu.VMEM((2, rows, width), BF16), pltpu.VMEM((2, rows, width), BF16),
                     pltpu.VMEM((2, rows, value_width), BF16), pltpu.SemaphoreType.DMA, pltpu.SemaphoreType.DMA((2, 2))],
            flops=flops, moved=2**24, name="backward",
        )(info, arrived, ends[min(tick, micro - 1)], on_chip(turned[0]), on_chip(turned[1]), sv, so, gains, *in_hbm(sources))

    up_routes = [(source, source + 2) for source in range(section_count - 2)]
    down_routes = [(source + 2, source) for source in range(section_count - 2)]
    empty = jnp.zeros((rows, width), BF16)
    sent_f, sent_b, stored, backs = [], [], [], []
    for tick in range(2 * ticks - micro + 1):
        if tick < ticks:
            out, kept = forward(tick, sent_f[tick - SKEW] if tick >= SKEW else empty)
            stored.append(kept)
            sent_f.append(lax.ppermute(out, "section", up_routes) if tick < ticks - SKEW else None)
            for first, late in ((1, True), (ticks - 6, False)):
                which = tick - first
                if 0 <= which < 2:
                    turn(which, late, lax.optimization_barrier((unorder, out))[0])
                    if tick + 1 >= SKEW:
                        at = tick + 1 - SKEW
                        sent_f[at], turned[which] = lax.optimization_barrier((sent_f[at], turned[which]))
        back = tick - (ticks - micro + 1)
        if back >= 0:
            out, upstream, vgrad = backward(back, sent_b[back - SKEW] if back >= SKEW else empty, stored)
            backs.append((upstream, vgrad))
            sent_b.append(lax.ppermute(out, "section", down_routes) if back < ticks - SKEW else None)

    stored_all = [kept[1] for kept in stored] + [kept[2] for kept in stored]
    stored_all += [back[0] for back in backs] + [back[1] for back in backs]
    sums = kernel_call(
        lambda *refs: grads_kernel(micro, stages, ticks, *refs),
        (jax.ShapeDtypeStruct((2, groups_v, value_width), F32), jax.ShapeDtypeStruct((2, groups_o, width), F32)),
        [SMEM] + [HBM] * len(stored_all), (VMEM, VMEM),
        scratch=[pltpu.VMEM((2, micro) + shape, BF16) for shape in (uv_shape[1:], uo_shape[1:], (rows, width), (rows, value_width))]
        + [pltpu.SemaphoreType.DMA((2, micro, 4))],
        flops=10**7, moved=2**24, name="grads", vmem=24 * 2**20,
    )(info, *in_hbm(stored_all))

    total_v = sums[0].reshape(2, groups_v, dp_count, -1).transpose(0, 2, 1, 3).reshape(2, dp_count, -1)
    total_o = sums[1].reshape(2, groups_o, dp_count, -1).transpose(0, 2, 1, 3).reshape(2, dp_count, -1)
    total = scatter_sums(jnp.concatenate([total_v, total_o], axis=2), side)
    return total[:count_v].reshape(steps_v.shape), total[count_v:].reshape(steps_o.shape)


def solution(mesh):
    return jax.shard_map(
        on_device,
        mesh=mesh,
        in_specs=(
            P(None, "dp", "section"),
            P(None, "dp", "section"),
            P("section", None, None),
            P("section", None, None),
            P("section", None, "dp"),
            P("section", None, None),
            P("section", None, None),
            P("section", None, "dp"),
            P("section", None),
        ),
        out_specs=(P("section", None, "dp"), P("section", None, "dp")),
        check_vma=False,
    )
```

```python
import jax
import jax.numpy as jnp
from jax import lax
from jax.experimental import pallas as pl
from jax.experimental.pallas import tpu as pltpu
from jax.sharding import PartitionSpec as P

F32, BF16, I32, F8 = jnp.float32, jnp.bfloat16, jnp.int32, jnp.float8_e4m3fn
GROUP = 128
LANES = 128
VMEM_BYTES = 12 * 2**20
STEP_V_MAX = 0.0144
STEP_O_MAX = 0.0575
F8_TOP = 400.0
SKEW = 2
LATE_STAGE = 4


def pair_words(words):
    rows, cols = words.shape
    shaped = words.reshape(rows // 16, 2, 8, cols)
    return (shaped[:, 0] | (shaped[:, 1] << 16)).reshape(rows // 2, cols)


def order_matrices():
    place = jnp.arange(LANES, dtype=I32)
    field, row = place // 8, place % 8
    natural = jnp.where(field < 8, 8 * row + field, 64 + 8 * row + field - 8)
    gather = (jnp.arange(LANES, dtype=I32)[:, None] == natural[None, :]).astype(BF16)
    return gather, gather.T


def centred_planes(words, zeros):
    planes = []
    for field in range(16):
        part = lax.shift_right_logical(words, jnp.int32(2 * field))
        if field < 15:
            part = part & 3
        planes.append(part.astype(F32) - zeros)
    return jnp.concatenate(planes, axis=0)


def unpack_part(place, v_ref, o_ref, v_at, o_at, qv_ref, qo_ref):
    groups_v, groups_o = qv_ref.shape[1] // GROUP, qo_ref.shape[1] // GROUP
    cols_v = pl.ds(v_at, v_ref.shape[1])

    def v_group(group, carry):
        words = v_ref[pl.ds(pl.multiple_of(group * 8, 8), 8), :]
        zeros = v_ref[pl.ds(groups_v * 8 + group, 1), :].astype(F32)
        at = pl.ds(pl.multiple_of(group * GROUP, GROUP), GROUP)
        qv_ref[place, at, cols_v] = centred_planes(words, zeros).astype(BF16).astype(F8)
        return carry

    lax.fori_loop(0, groups_v, v_group, 0, unroll=4)

    def o_cols(block, carry):
        cols = pl.ds(pl.multiple_of(block * 512, 512), 512)
        cols_o = pl.ds(pl.multiple_of(o_at + block * 512, 512), 512)
        for group in range(groups_o):
            words = o_ref[group * 8:group * 8 + 8, cols]
            zeros = o_ref[groups_o * 8 + group:groups_o * 8 + group + 1, cols].astype(F32)
            at = slice(group * GROUP, (group + 1) * GROUP)
            qo_ref[place, at, cols_o] = centred_planes(words, zeros).astype(BF16).astype(F8)
        return carry

    lax.fori_loop(0, o_ref.shape[1] // 512, o_cols, 0)


def unpack_own_kernel(v_ref, o_ref, qv_ref, qo_ref):
    unpack_part(0, v_ref, o_ref, 0, 0, qv_ref, qo_ref)


def unpack_far_kernel(info_ref, v_same, v_other, o_same, o_other, own_sv, far_sv, own_so, far_so, qv_in, qo_in,
                      qv_ref, qo_ref, sv_ref, so_ref, gain_ref):
    core = info_ref[2]
    groups_o = so_ref.shape[1]
    for place, (sv, so) in enumerate(((own_sv, own_so), (far_sv, far_so))):
        sv_ref[place] = sv[...]
        so_ref[place] = so[:groups_o, :]
        gain_ref[place] = so[groups_o:, :]
    for v_ref, o_ref, half in ((v_same, o_same, core), (v_other, o_other, 1 - core)):
        v_at = pl.multiple_of(half * v_ref.shape[1], v_ref.shape[1])
        o_at = pl.multiple_of(half * o_ref.shape[1], o_ref.shape[1])
        unpack_part(1, v_ref, o_ref, v_at, o_at, qv_ref, qo_ref)


def turn_v_kernel(late, place, info_ref, unorder_ref, qv_ref, *rest):
    turned_ref = rest[-1]

    @pl.when((info_ref[0] >= LATE_STAGE) == late)
    def _():
        unorder = unorder_ref[...]

        def group_turn(group, carry):
            at = pl.ds(pl.multiple_of(group * GROUP, GROUP), GROUP)
            turned_ref[place, :, at] = lax.dot_general(
                qv_ref[place, at, :].astype(BF16), unorder, (((0,), (0,)), ((), ())),
                preferred_element_type=F32).astype(F8)
            return carry

        lax.fori_loop(0, qv_ref.shape[1] // GROUP, group_turn, 0, unroll=8)


def turn_o_kernel(late, place, info_ref, unorder_ref, qo_ref, *rest):
    turned_ref = rest[-1]

    @pl.when((info_ref[0] >= LATE_STAGE) == late)
    def _():
        unorder = unorder_ref[...]

        def cols_turn(block, carry):
            at = pl.ds(pl.multiple_of(block * 512, 512), 512)
            for group in range(qo_ref.shape[1] // GROUP):
                span = slice(group * GROUP, (group + 1) * GROUP)
                turned_ref[place, at, span] = lax.dot_general(
                    qo_ref[place, span, at].astype(BF16), unorder, (((0,), (0,)), ((), ())),
                    preferred_element_type=F32).astype(F8)
            return carry

        lax.fori_loop(0, qo_ref.shape[2] // 512, cols_turn, 0, unroll=2)


def split8(value):
    high = value.astype(F8).astype(F32)
    return high, (value - high) * 16.0


def merge8(out, start):
    return out[start:start + 16] + out[start + 16:start + 32] * 0.0625


def diag_pair(first, second):
    zero = jnp.zeros_like(first)
    return jnp.concatenate(
        [jnp.concatenate([first, zero], axis=1), jnp.concatenate([zero, second], axis=1)], axis=0
    )


def blocks_down(value):
    return jnp.concatenate([value[:, at:at + LANES] for at in range(0, value.shape[1], LANES)], axis=0)


def blocks_across(value, rows):
    return jnp.concatenate([value[at:at + rows] for at in range(0, value.shape[0], rows)], axis=1)


def row_inverse(states):
    return lax.rsqrt(jnp.mean(states * states, axis=-1, keepdims=True) + 1e-05)


def forward_layer(states, qv, qo, sv, so, gain_row, order, uv_ref, uo_ref, halfway):
    rows, width = states.shape
    normed = (states * row_inverse(states) * gain_row).astype(BF16)
    high, low = split8(jnp.dot(blocks_down(normed), order, preferred_element_type=F32))
    groups = width // GROUP
    tiles = jnp.concatenate(
        [high.reshape(groups, rows, LANES), low.reshape(groups, rows, LANES)], axis=1
    ).astype(F8)
    total = jnp.zeros((rows, sv.shape[1]), F32)
    for group in range(0, groups, 2):
        out = jnp.dot(
            diag_pair(tiles[group], tiles[group + 1]),
            qv[group * GROUP:(group + 2) * GROUP, :],
            preferred_element_type=F32,
        )
        for place in range(2):
            unit = merge8(out, 32 * place)
            uv_ref[group + place] = unit.astype(BF16)
            total = total + unit * sv[group + place:group + place + 1, :]
    halfway()
    values = total.astype(BF16)
    ordered = jnp.dot(blocks_down(values), order, preferred_element_type=F32)
    peak = jnp.maximum(jnp.max(jnp.abs(values.astype(F32)), axis=-1, keepdims=True), 1e-37)
    groups_o = values.shape[1] // GROUP
    tiles_o = []
    for group in range(groups_o):
        high, low = split8(ordered[group * rows:(group + 1) * rows] * (1.0 / peak) * F8_TOP)
        tiles_o.append(jnp.concatenate([high, low], axis=0).astype(F8))
    pairs = [diag_pair(tiles_o[group], tiles_o[group + 1]) for group in range(0, groups_o, 2)]
    back = peak * (1.0 / F8_TOP)
    updated = []
    for at in range(0, width, 512):
        moved = states[:, at:at + 512]
        for index, pair in enumerate(pairs):
            out = jnp.dot(pair, qo[index * 256:(index + 1) * 256, at:at + 512], preferred_element_type=F32)
            for place in range(2):
                group = 2 * index + place
                unit = merge8(out, 32 * place) * back
                uo_ref[group, :, at:at + 512] = unit.astype(BF16)
                moved = moved + unit * so[group:group + 1, at:at + 512]
        updated.append(moved.astype(BF16))
    return jnp.concatenate(updated, axis=1)


def forward_kernel(tick, micro, info_ref, arrived_ref, fresh_ref, qv_ref, qo_ref, sv_ref, so_ref, gain_ref, order_ref,
                   out_ref, states_hbm, uv_hbm, uo_hbm, states_ref, uv_ref, uo_ref, sems):
    z, swap = info_ref[0], info_ref[1]
    position = tick - SKEW * z

    def copies(index):
        return [
            pltpu.make_async_copy(here.at[index], there.at[index], sems.at[index, at])
            for at, (here, there) in enumerate(((states_ref, states_hbm), (uv_ref, uv_hbm), (uo_ref, uo_hbm)))
        ]

    def start(index, places):
        for copy in copies(index)[places]:
            copy.start()

    @pl.when((position >= 0) & (position < micro))
    def _():
        out_ref[...] = jnp.where(z == 0, fresh_ref[...], arrived_ref[...])
        order = order_ref[...]

        def layer(index, carry):
            place = index ^ swap
            states = out_ref[...]
            states_ref[index] = states
            out_ref[...] = forward_layer(
                states.astype(F32), qv_ref.at[place], qo_ref.at[place], sv_ref.at[place], so_ref.at[place],
                gain_ref[place], order, uv_ref.at[index], uo_ref.at[index], lambda: start(index, slice(0, 2)))
            start(index, slice(2, 3))
            return carry

        lax.fori_loop(0, 2, layer, 0)
        for index in range(2):
            for copy in copies(index):
                copy.wait()


def backward_layer(upstream, states, tv, to, sv, so, gain_row):
    rows, width = upstream.shape
    peak = jnp.maximum(jnp.max(jnp.abs(upstream), axis=-1, keepdims=True), 1e-37)
    scaled = upstream * (1.0 / peak) * (F8_TOP / STEP_O_MAX)
    groups_o = so.shape[0]
    found = []
    for group in range(0, groups_o, 2):
        parts = []
        for place in range(2):
            high, low = split8(scaled * so[group + place:group + place + 1, :])
            parts += [high, low]
        left = jnp.concatenate(parts, axis=0).astype(F8)
        out = jnp.dot(left, to[:, group * GROUP:(group + 2) * GROUP], preferred_element_type=F32)
        found += [merge8(out[:, :LANES], 0), merge8(out[:, LANES:], 32)]
    vgrad = (jnp.concatenate(found, axis=1) * (peak * (STEP_O_MAX / F8_TOP))).astype(BF16).astype(F32)
    peak = jnp.maximum(jnp.max(jnp.abs(vgrad), axis=-1, keepdims=True), 1e-37)
    scaled = vgrad * (1.0 / peak) * (F8_TOP / STEP_V_MAX)
    found = []
    for group in range(0, width // GROUP, 2):
        parts = []
        for place in range(2):
            high, low = split8(scaled * sv[group + place:group + place + 1, :])
            parts += [high, low]
        left = jnp.concatenate(parts, axis=0).astype(F8)
        out = jnp.dot(left, tv[:, group * GROUP:(group + 2) * GROUP], preferred_element_type=F32)
        found += [merge8(out[:, :LANES], 0), merge8(out[:, LANES:], 32)]
    ngrad = jnp.concatenate(found, axis=1) * gain_row * (peak * (STEP_V_MAX / F8_TOP))
    inverse = row_inverse(states)
    mixed = jnp.mean(ngrad * states, axis=-1, keepdims=True)
    moved = upstream + inverse * ngrad - states * (inverse * inverse * inverse) * mixed
    return moved.astype(BF16), vgrad.astype(BF16)


def backward_kernel(tick, micro, stages, places, info_ref, arrived_ref, fresh_ref, tv_ref, to_ref, sv_ref, so_ref, gain_ref,
                    *rest):
    stored = rest[:len(places)]
    out_ref, upstream_hbm, vgrad_hbm, states_ref, upstream_ref, vgrad_ref, sem, sems = rest[len(places):]
    z, swap = info_ref[0], info_ref[1]
    position = tick - SKEW * (stages - 1 - z)

    def upstream_copy(index):
        return pltpu.make_async_copy(upstream_ref.at[index], upstream_hbm.at[index], sems.at[index, 0])

    def vgrad_copy(index):
        return pltpu.make_async_copy(vgrad_ref.at[index], vgrad_hbm.at[index], sems.at[index, 1])

    @pl.when((position >= 0) & (position < micro))
    def _():
        for place_at, source in zip(places, stored):

            @pl.when(z == place_at)
            def _():
                pltpu.make_async_copy(source, states_ref, sem).start()

        out_ref[...] = jnp.where(z == stages - 1, fresh_ref[...], arrived_ref[...])
        pltpu.make_async_copy(stored[0], states_ref, sem).wait()

        def layer(step, carry):
            index = 1 - step
            place = index ^ swap
            upstream = out_ref[...]
            upstream_ref[index] = upstream
            upstream_copy(index).start()
            moved, vgrad = backward_layer(
                upstream.astype(F32), states_ref[index].astype(F32), tv_ref.at[place], to_ref.at[place],
                sv_ref.at[place], so_ref.at[place], gain_ref[place])
            out_ref[...] = moved
            vgrad_ref[index] = vgrad
            vgrad_copy(index).start()
            return carry

        lax.fori_loop(0, 2, layer, 0)
        for index in range(2):
            upstream_copy(index).wait()
            vgrad_copy(index).wait()


def grads_kernel(micro, stages, ticks, info_ref, *rest):
    kinds = [rest[kind * ticks:(kind + 1) * ticks] for kind in range(4)]
    gv_ref, go_ref, uv_ref, uo_ref, up_ref, vg_ref, sems = rest[4 * ticks:]
    targets = (uv_ref, uo_ref, up_ref, vg_ref)
    z, swap = info_ref[0], info_ref[1]
    for place in range(stages):

        @pl.when(z == place)
        def _():
            for index in range(2):
                for kind, step in [(kind, step) for kind in (3, 0, 2, 1) for step in range(micro)]:
                    at = step + SKEW * (place if kind < 2 else stages - 1 - place)
                    pltpu.make_async_copy(
                        kinds[kind][at].at[index], targets[kind].at[index, step], sems.at[index, step, kind]).start()

    def arrive(index, chosen):
        for step in range(micro):
            for kind in chosen:
                pltpu.make_async_copy(
                    kinds[kind][0].at[index], targets[kind].at[index, step], sems.at[index, step, kind]).wait()

    for index in range(2):
        target = index ^ swap
        arrive(index, (0, 3))
        vgrads = [vg_ref[index, step].astype(F32) for step in range(micro)]

        def groups_v(block, carry):
            sums = []
            for at in range(8):
                total = uv_ref[index, 0, block * 8 + at].astype(F32) * vgrads[0]
                for step in range(1, micro):
                    total = total + uv_ref[index, step, block * 8 + at].astype(F32) * vgrads[step]
                sums.append(jnp.sum(total, axis=0, keepdims=True))
            gv_ref[target, pl.ds(pl.multiple_of(block * 8, 8), 8), :] = jnp.concatenate(sums, axis=0)
            return carry

        lax.fori_loop(0, gv_ref.shape[1] // 8, groups_v, 0)

        arrive(index, (1, 2))

        def cols_o(block, carry):
            cols = pl.ds(pl.multiple_of(block * 512, 512), 512)
            ups = [up_ref[index, step, :, cols].astype(F32) for step in range(micro)]
            sums = []
            for group in range(go_ref.shape[1]):
                total = uo_ref[index, 0, group, :, cols].astype(F32) * ups[0]
                for step in range(1, micro):
                    total = total + uo_ref[index, step, group, :, cols].astype(F32) * ups[step]
                sums.append(jnp.sum(total, axis=0, keepdims=True))
            go_ref[target, :, cols] = jnp.concatenate(sums, axis=0)
            return carry

        lax.fori_loop(0, go_ref.shape[2] // 512, cols_o, 0)


VMEM = pl.BlockSpec(memory_space=pltpu.VMEM)
SMEM = pl.BlockSpec(memory_space=pltpu.SMEM)
HBM = pl.BlockSpec(memory_space=pltpu.HBM)


def on_chip(value):
    return pltpu.with_memory_space_constraint(value, pltpu.VMEM)


def in_hbm(values):
    return [pltpu.with_memory_space_constraint(value, pltpu.HBM) for value in values]


def kernel_call(body, outs, in_specs, out_specs, scratch=(), aliases=None, flops=0, moved=0, name=None, vmem=VMEM_BYTES):
    return pl.pallas_call(
        body,
        out_shape=outs,
        in_specs=in_specs,
        out_specs=out_specs,
        scratch_shapes=list(scratch),
        input_output_aliases=aliases or {},
        compiler_params=pltpu.CompilerParams(vmem_limit_bytes=vmem),
        cost_estimate=pl.CostEstimate(flops=flops, bytes_accessed=moved, transcendentals=0),
        name=name,
    )


def fixed_swap(value, axis, bit):
    count = lax.axis_size(axis)
    return lax.ppermute(value, axis, [(source, source ^ bit) for source in range(count)])


def half_codes(words, core):
    low, high = jnp.split(words, 2, axis=1)
    return fixed_swap(jnp.where(core == 0, low, high), "section", 1)


def ends_rows(hidden_in, cotangent, stages):
    micro, rows, part = hidden_in.shape
    half = micro // 2
    hidden = hidden_in.reshape(2, half, rows, part).transpose(1, 0, 2, 3)
    last = cotangent.reshape(2, half, rows, part).transpose(1, 0, 2, 3)
    pieces = jnp.concatenate([hidden, last[::-1]]).reshape(4 * half, rows, part)
    found = lax.all_to_all(pieces, "section", 0, 0)
    found = found.transpose(1, 0, 2).reshape(rows, 4 * half * part)
    routes = []
    for place in range(1, half):
        for side_at in range(2):
            routes.append((2 * place + side_at, 2 * (place - 1) + side_at))
            routes.append((2 * (stages - 1 - place) + side_at, 2 * (stages - place) + side_at))
    ends = [found]
    for _ in range(half - 1):
        ends.append(lax.ppermute(ends[-1], "section", routes))
    return ends


def gather_steps(value):
    count = lax.axis_size("dp")
    return lax.all_to_all(jnp.broadcast_to(value[None], (count,) + value.shape), "dp", 0, 0)


def scatter_sums(value):
    total = value[0] + fixed_swap(value[1].astype(BF16), "section", 1).astype(F32)
    return jnp.sum(lax.all_to_all(total.astype(BF16), "dp", 0, 0).astype(F32), axis=0)


def on_device(hidden_in, cotangent, codes_v, zeros_v, steps_v, codes_o, zeros_o, steps_o, gain):
    section_id = lax.axis_index("section")
    section_count = lax.axis_size("section")
    dp_count = lax.axis_size("dp")
    z, side = section_id // 2, section_id % 2
    stages = section_count // 2
    micro = hidden_in.shape[0] // 2
    rows = hidden_in.shape[1]
    width, value_width = gain.shape[1], codes_v.shape[2]
    groups_v, groups_o = zeros_v.shape[1], zeros_o.shape[1]

    own_v = jnp.concatenate([pair_words(codes_v[0]), zeros_v[0]], axis=0)
    own_o = jnp.concatenate([pair_words(codes_o[0]), zeros_o[0]], axis=0)
    core = lax.axis_index("dp") % 2
    same_v, same_o = half_codes(own_v, core), half_codes(own_o, core)
    ends = ends_rows(hidden_in, cotangent, stages)
    count_v, count_o = steps_v.size, steps_o.size
    steps = gather_steps(jnp.concatenate([steps_v.reshape(-1), steps_o.reshape(-1)]).astype(BF16)).astype(F32)
    own_sv = steps[:, :count_v].reshape(dp_count, groups_v, -1).transpose(1, 0, 2).reshape(groups_v, value_width)
    own_so = steps[:, count_v:].reshape(dp_count, groups_o, -1).transpose(1, 0, 2).reshape(groups_o, width)
    own_so = jnp.concatenate([own_so, gain], axis=0)
    far_sv, far_so = fixed_swap(own_sv, "section", 1), fixed_swap(own_so, "section", 1)
    order, unorder = order_matrices()
    info = jnp.stack([z, side, core]).astype(I32)
    own_v, own_o, own_sv, own_so, same_v, same_o, order, unorder, info, ends[0] = lax.optimization_barrier(
        (own_v, own_o, own_sv, own_so, same_v, same_o, order, unorder, info, ends[0]))
    other_v, other_o = fixed_swap(same_v, "dp", 1), fixed_swap(same_o, "dp", 1)

    q_shapes = (pltpu.VMEM((2, width, value_width), F8), pltpu.VMEM((2, value_width, width), F8))
    qv, qo = kernel_call(
        unpack_own_kernel, q_shapes, [VMEM] * 2, (VMEM, VMEM), flops=10**8, moved=2**22, name="unpack_own",
    )(own_v, own_o)
    qv, qo, sv, so, gains = kernel_call(
        unpack_far_kernel,
        q_shapes + tuple(jax.ShapeDtypeStruct(shape, F32) for shape in (
            (2, groups_v, value_width), (2, groups_o, width), (2, 1, width))),
        [SMEM] + [VMEM] * 10, (VMEM,) * 5, aliases={9: 0, 10: 1}, flops=10**8, moved=2**22, name="unpack_far",
    )(info, same_v, other_v, same_o, other_o, own_sv, far_sv, own_so, far_so, on_chip(qv), on_chip(qo))
    qv, qo = on_chip(qv), on_chip(qo)

    t_shapes = (pltpu.VMEM((2, value_width, width), F8), pltpu.VMEM((2, width, value_width), F8))
    turned = [None, None]

    def turn(which, late, place, unorder):
        body = (turn_v_kernel, turn_o_kernel)[which]
        known = [] if turned[which] is None else [on_chip(turned[which])]
        turned[which] = kernel_call(
            lambda *refs: body(late, place, *refs), t_shapes[which], [SMEM] + [VMEM] * (2 + len(known)), VMEM,
            aliases={3: 0} if known else {}, flops=10**8, moved=2**22, name="turn",
        )(info, unorder, (qv, qo)[which], *known)

    uv_shape, uo_shape = (2, groups_v, rows, value_width), (2, groups_o, rows, width)
    stored_shapes = [(2, rows, width), uv_shape, uo_shape]
    flops = 4 * 2 * rows * width * value_width * 2
    last = stages - 1
    ticks = micro + SKEW * last

    def forward(tick, arrived, info):
        done = kernel_call(
            lambda *refs: forward_kernel(tick, micro, *refs),
            (jax.ShapeDtypeStruct((rows, width), BF16),) + tuple(pltpu.HBM(shape, BF16) for shape in stored_shapes),
            [SMEM] + [VMEM] * 8, (VMEM, HBM, HBM, HBM),
            scratch=[pltpu.VMEM(shape, BF16) for shape in stored_shapes] + [pltpu.SemaphoreType.DMA((2, 3))],
            flops=flops, moved=2**24, name="forward",
        )(info, arrived, ends[min(tick, micro - 1)], qv, qo, sv, so, gains, order)
        return done[0], done[1:]

    def backward(tick, arrived, stored, info):
        places = [place for place in range(stages) if 0 <= tick - SKEW * (last - place) < micro]
        sources = [stored[SKEW * place + tick - SKEW * (last - place)][0] for place in places]
        return kernel_call(
            lambda *refs: backward_kernel(tick, micro, stages, places, *refs),
            (jax.ShapeDtypeStruct((rows, width), BF16), pltpu.HBM((2, rows, width), BF16),
             pltpu.HBM((2, rows, value_width), BF16)),
            [SMEM] + [VMEM] * 7 + [HBM] * len(places), (VMEM, HBM, HBM),
            scratch=[pltpu.VMEM((2, rows, width), BF16), pltpu.VMEM((2, rows, width), BF16),
                     pltpu.VMEM((2, rows, value_width), BF16), pltpu.SemaphoreType.DMA, pltpu.SemaphoreType.DMA((2, 2))],
            flops=flops, moved=2**24, name="backward",
        )(info, arrived, ends[min(tick, micro - 1)], on_chip(turned[0]), on_chip(turned[1]), sv, so, gains, *in_hbm(sources))

    up_routes = [(source, source + 2) for source in range(section_count - 2)]
    down_routes = [(source + 2, source) for source in range(section_count - 2)]
    empty = jnp.zeros((rows, width), BF16)
    sent_f, sent_b, stored, backs = [], [], [], []
    for tick in range(2 * ticks - micro + 1):
        if tick < ticks:
            out, kept = forward(tick, sent_f[tick - SKEW] if tick >= SKEW else empty, info)
            stored.append(kept)
            sent_f.append(lax.ppermute(out, "section", up_routes) if tick < ticks - SKEW else None)
            for first, late in ((1, True), (ticks - 7, False)):
                if 0 <= tick - first < 4:
                    which, place = divmod(tick - first, 2)
                    turn(which, late, place, lax.optimization_barrier((unorder, out))[0])
                    info, turned[which] = lax.optimization_barrier((info, turned[which]))
        back = tick - (ticks - micro + 1)
        if back >= 0:
            out, upstream, vgrad = backward(back, sent_b[back - SKEW] if back >= SKEW else empty, stored, info)
            backs.append((upstream, vgrad))
            sent_b.append(lax.ppermute(out, "section", down_routes) if back < ticks - SKEW else None)

    stored_all = [kept[1] for kept in stored] + [kept[2] for kept in stored]
    stored_all += [back[0] for back in backs] + [back[1] for back in backs]
    sums = kernel_call(
        lambda *refs: grads_kernel(micro, stages, ticks, *refs),
        (jax.ShapeDtypeStruct((2, groups_v, value_width), F32), jax.ShapeDtypeStruct((2, groups_o, width), F32)),
        [SMEM] + [HBM] * len(stored_all), (VMEM, VMEM),
        scratch=[pltpu.VMEM((2, micro) + shape, BF16) for shape in (uv_shape[1:], uo_shape[1:], (rows, width), (rows, value_width))]
        + [pltpu.SemaphoreType.DMA((2, micro, 4))],
        flops=10**7, moved=2**24, name="grads", vmem=24 * 2**20,
    )(info, *in_hbm(stored_all))

    total_v = sums[0].reshape(2, groups_v, dp_count, -1).transpose(0, 2, 1, 3).reshape(2, dp_count, -1)
    total_o = sums[1].reshape(2, groups_o, dp_count, -1).transpose(0, 2, 1, 3).reshape(2, dp_count, -1)
    total = scatter_sums(jnp.concatenate([total_v, total_o], axis=2))
    return total[:count_v].reshape(steps_v.shape), total[count_v:].reshape(steps_o.shape)


def solution(mesh):
    return jax.shard_map(
        on_device,
        mesh=mesh,
        in_specs=(
            P(None, "dp", "section"),
            P(None, "dp", "section"),
            P("section", None, None),
            P("section", None, None),
            P("section", None, "dp"),
            P("section", None, None),
            P("section", None, None),
            P("section", None, "dp"),
            P("section", None),
        ),
        out_specs=(P("section", None, "dp"), P("section", None, "dp")),
        check_vma=False,
    )
```

```python
import jax
import jax.numpy as jnp
from jax import lax
from jax.experimental import pallas as pl
from jax.experimental.pallas import tpu as pltpu
from jax.sharding import PartitionSpec as P

F32, BF16, I32, F8 = jnp.float32, jnp.bfloat16, jnp.int32, jnp.float8_e4m3fn
GROUP = 128
LANES = 128
VMEM_BYTES = 12 * 2**20
STEP_V_MAX = 0.0144
STEP_O_MAX = 0.0575
F8_TOP = 400.0
SKEW = 2
LATE_STAGE = 4


def pair_words(words):
    rows, cols = words.shape
    shaped = words.reshape(rows // 16, 2, 8, cols)
    return (shaped[:, 0] | (shaped[:, 1] << 16)).reshape(rows // 2, cols)


def order_matrices():
    place = jnp.arange(LANES, dtype=I32)
    field, row = place // 8, place % 8
    natural = jnp.where(field < 8, 8 * row + field, 64 + 8 * row + field - 8)
    gather = (jnp.arange(LANES, dtype=I32)[:, None] == natural[None, :]).astype(BF16)
    return gather, gather.T


def centred_planes(words, zeros):
    planes = []
    for field in range(16):
        part = lax.shift_right_logical(words, jnp.int32(2 * field))
        if field < 15:
            part = part & 3
        planes.append(part.astype(F32) - zeros)
    return jnp.concatenate(planes, axis=0)


def unpack_part(place, v_ref, o_ref, v_at, o_at, qv_ref, qo_ref):
    groups_v, groups_o = qv_ref.shape[1] // GROUP, qo_ref.shape[1] // GROUP
    cols_v = pl.ds(v_at, v_ref.shape[1])

    def v_group(group, carry):
        words = v_ref[pl.ds(pl.multiple_of(group * 8, 8), 8), :]
        zeros = v_ref[pl.ds(groups_v * 8 + group, 1), :].astype(F32)
        at = pl.ds(pl.multiple_of(group * GROUP, GROUP), GROUP)
        qv_ref[place, at, cols_v] = centred_planes(words, zeros).astype(BF16).astype(F8)
        return carry

    lax.fori_loop(0, groups_v, v_group, 0, unroll=4)

    def o_cols(block, carry):
        cols = pl.ds(pl.multiple_of(block * 512, 512), 512)
        cols_o = pl.ds(pl.multiple_of(o_at + block * 512, 512), 512)
        for group in range(groups_o):
            words = o_ref[group * 8:group * 8 + 8, cols]
            zeros = o_ref[groups_o * 8 + group:groups_o * 8 + group + 1, cols].astype(F32)
            at = slice(group * GROUP, (group + 1) * GROUP)
            qo_ref[place, at, cols_o] = centred_planes(words, zeros).astype(BF16).astype(F8)
        return carry

    lax.fori_loop(0, o_ref.shape[1] // 512, o_cols, 0)


def unpack_own_kernel(v_ref, o_ref, qv_ref, qo_ref):
    unpack_part(0, v_ref, o_ref, 0, 0, qv_ref, qo_ref)


def unpack_far_kernel(info_ref, v_same, v_other, o_same, o_other, own_steps, far_steps, qv_in, qo_in,
                      qv_ref, qo_ref, sv_ref, so_ref, gain_ref):
    core = info_ref[2]
    groups_v, value_width = sv_ref.shape[1:]
    groups_o, width = so_ref.shape[1:]
    per_row = width // value_width
    rows_v = groups_v // per_row
    for place, packed in enumerate((own_steps, far_steps)):
        for group in range(groups_v):
            row, at = group // per_row, (group % per_row) * value_width
            sv_ref[place, group:group + 1, :] = packed[row:row + 1, at:at + value_width]
        so_ref[place] = packed[rows_v:rows_v + groups_o, :]
        gain_ref[place] = packed[rows_v + groups_o:, :]
    for v_ref, o_ref, half in ((v_same, o_same, core), (v_other, o_other, 1 - core)):
        v_at = pl.multiple_of(half * v_ref.shape[1], v_ref.shape[1])
        o_at = pl.multiple_of(half * o_ref.shape[1], o_ref.shape[1])
        unpack_part(1, v_ref, o_ref, v_at, o_at, qv_ref, qo_ref)


def turn_v_kernel(late, place, info_ref, unorder_ref, qv_ref, *rest):
    turned_ref = rest[-1]

    @pl.when((info_ref[0] >= LATE_STAGE) == late)
    def _():
        unorder = unorder_ref[...]

        def group_turn(group, carry):
            at = pl.ds(pl.multiple_of(group * GROUP, GROUP), GROUP)
            turned_ref[place, :, at] = lax.dot_general(
                qv_ref[place, at, :].astype(BF16), unorder, (((0,), (0,)), ((), ())),
                preferred_element_type=F32).astype(F8)
            return carry

        lax.fori_loop(0, qv_ref.shape[1] // GROUP, group_turn, 0, unroll=8)


def turn_o_kernel(late, place, info_ref, unorder_ref, qo_ref, *rest):
    turned_ref = rest[-1]

    @pl.when((info_ref[0] >= LATE_STAGE) == late)
    def _():
        unorder = unorder_ref[...]

        def cols_turn(block, carry):
            at = pl.ds(pl.multiple_of(block * 512, 512), 512)
            for group in range(qo_ref.shape[1] // GROUP):
                span = slice(group * GROUP, (group + 1) * GROUP)
                turned_ref[place, at, span] = lax.dot_general(
                    qo_ref[place, span, at].astype(BF16), unorder, (((0,), (0,)), ((), ())),
                    preferred_element_type=F32).astype(F8)
            return carry

        lax.fori_loop(0, qo_ref.shape[2] // 512, cols_turn, 0, unroll=2)


def split8(value):
    high = value.astype(F8).astype(F32)
    return high, (value - high) * 16.0


def merge8(out, start):
    return out[start:start + 16] + out[start + 16:start + 32] * 0.0625


def diag_pair(first, second):
    zero = jnp.zeros_like(first)
    return jnp.concatenate(
        [jnp.concatenate([first, zero], axis=1), jnp.concatenate([zero, second], axis=1)], axis=0
    )


def blocks_down(value):
    return jnp.concatenate([value[:, at:at + LANES] for at in range(0, value.shape[1], LANES)], axis=0)


def blocks_across(value, rows):
    return jnp.concatenate([value[at:at + rows] for at in range(0, value.shape[0], rows)], axis=1)


def row_inverse(states):
    return lax.rsqrt(jnp.mean(states * states, axis=-1, keepdims=True) + 1e-05)


def forward_layer(states, qv, qo, sv, so, gain_row, order, uv_ref, uo_ref, halfway):
    rows, width = states.shape
    normed = (states * row_inverse(states) * gain_row).astype(BF16)
    high, low = split8(jnp.dot(blocks_down(normed), order, preferred_element_type=F32))
    groups = width // GROUP
    tiles = jnp.concatenate(
        [high.reshape(groups, rows, LANES), low.reshape(groups, rows, LANES)], axis=1
    ).astype(F8)
    total = jnp.zeros((rows, sv.shape[1]), F32)
    for group in range(0, groups, 2):
        out = jnp.dot(
            diag_pair(tiles[group], tiles[group + 1]),
            qv[group * GROUP:(group + 2) * GROUP, :],
            preferred_element_type=F32,
        )
        for place in range(2):
            unit = merge8(out, 32 * place)
            uv_ref[group + place] = unit.astype(BF16)
            total = total + unit * sv[group + place:group + place + 1, :]
    halfway()
    values = total.astype(BF16)
    ordered = jnp.dot(blocks_down(values), order, preferred_element_type=F32)
    peak = jnp.maximum(jnp.max(jnp.abs(values.astype(F32)), axis=-1, keepdims=True), 1e-37)
    groups_o = values.shape[1] // GROUP
    tiles_o = []
    for group in range(groups_o):
        high, low = split8(ordered[group * rows:(group + 1) * rows] * (1.0 / peak) * F8_TOP)
        tiles_o.append(jnp.concatenate([high, low], axis=0).astype(F8))
    pairs = [diag_pair(tiles_o[group], tiles_o[group + 1]) for group in range(0, groups_o, 2)]
    back = peak * (1.0 / F8_TOP)
    updated = []
    for at in range(0, width, 512):
        moved = states[:, at:at + 512]
        for index, pair in enumerate(pairs):
            out = jnp.dot(pair, qo[index * 256:(index + 1) * 256, at:at + 512], preferred_element_type=F32)
            for place in range(2):
                group = 2 * index + place
                unit = merge8(out, 32 * place) * back
                uo_ref[group, :, at:at + 512] = unit.astype(BF16)
                moved = moved + unit * so[group:group + 1, at:at + 512]
        updated.append(moved.astype(BF16))
    return jnp.concatenate(updated, axis=1)


def forward_kernel(tick, micro, info_ref, arrived_ref, fresh_ref, qv_ref, qo_ref, sv_ref, so_ref, gain_ref, order_ref,
                   out_ref, states_hbm, uv_hbm, uo_hbm, states_ref, uv_ref, uo_ref, sems):
    z, swap = info_ref[0], info_ref[1]
    position = tick - SKEW * z

    def copies(index):
        return [
            pltpu.make_async_copy(here.at[index], there.at[index], sems.at[index, at])
            for at, (here, there) in enumerate(((states_ref, states_hbm), (uv_ref, uv_hbm), (uo_ref, uo_hbm)))
        ]

    def start(index, places):
        for copy in copies(index)[places]:
            copy.start()

    @pl.when((position >= 0) & (position < micro))
    def _():
        out_ref[...] = jnp.where(z == 0, fresh_ref[...], arrived_ref[...])
        order = order_ref[...]

        def layer(index, carry):
            place = index ^ swap
            states = out_ref[...]
            states_ref[index] = states
            out_ref[...] = forward_layer(
                states.astype(F32), qv_ref.at[place], qo_ref.at[place], sv_ref.at[place], so_ref.at[place],
                gain_ref[place], order, uv_ref.at[index], uo_ref.at[index], lambda: start(index, slice(0, 2)))
            start(index, slice(2, 3))
            return carry

        lax.fori_loop(0, 2, layer, 0)
        for index in range(2):
            for copy in copies(index):
                copy.wait()


def backward_layer(upstream, states, tv, to, sv, so, gain_row):
    rows, width = upstream.shape
    peak = jnp.maximum(jnp.max(jnp.abs(upstream), axis=-1, keepdims=True), 1e-37)
    scaled = upstream * (1.0 / peak) * (F8_TOP / STEP_O_MAX)
    groups_o = so.shape[0]
    found = []
    for group in range(0, groups_o, 2):
        parts = []
        for place in range(2):
            high, low = split8(scaled * so[group + place:group + place + 1, :])
            parts += [high, low]
        left = jnp.concatenate(parts, axis=0).astype(F8)
        out = jnp.dot(left, to[:, group * GROUP:(group + 2) * GROUP], preferred_element_type=F32)
        found += [merge8(out[:, :LANES], 0), merge8(out[:, LANES:], 32)]
    vgrad = (jnp.concatenate(found, axis=1) * (peak * (STEP_O_MAX / F8_TOP))).astype(BF16).astype(F32)
    peak = jnp.maximum(jnp.max(jnp.abs(vgrad), axis=-1, keepdims=True), 1e-37)
    scaled = vgrad * (1.0 / peak) * (F8_TOP / STEP_V_MAX)
    found = []
    for group in range(0, width // GROUP, 2):
        parts = []
        for place in range(2):
            high, low = split8(scaled * sv[group + place:group + place + 1, :])
            parts += [high, low]
        left = jnp.concatenate(parts, axis=0).astype(F8)
        out = jnp.dot(left, tv[:, group * GROUP:(group + 2) * GROUP], preferred_element_type=F32)
        found += [merge8(out[:, :LANES], 0), merge8(out[:, LANES:], 32)]
    ngrad = jnp.concatenate(found, axis=1) * gain_row * (peak * (STEP_V_MAX / F8_TOP))
    inverse = row_inverse(states)
    mixed = jnp.mean(ngrad * states, axis=-1, keepdims=True)
    moved = upstream + inverse * ngrad - states * (inverse * inverse * inverse) * mixed
    return moved.astype(BF16), vgrad.astype(BF16)


def backward_kernel(tick, micro, stages, places, info_ref, arrived_ref, fresh_ref, tv_ref, to_ref, sv_ref, so_ref, gain_ref,
                    *rest):
    stored = rest[:len(places)]
    out_ref, upstream_hbm, vgrad_hbm, states_ref, upstream_ref, vgrad_ref, sem, sems = rest[len(places):]
    z, swap = info_ref[0], info_ref[1]
    position = tick - SKEW * (stages - 1 - z)

    def upstream_copy(index):
        return pltpu.make_async_copy(upstream_ref.at[index], upstream_hbm.at[index], sems.at[index, 0])

    def vgrad_copy(index):
        return pltpu.make_async_copy(vgrad_ref.at[index], vgrad_hbm.at[index], sems.at[index, 1])

    @pl.when((position >= 0) & (position < micro))
    def _():
        for place_at, source in zip(places, stored):

            @pl.when(z == place_at)
            def _():
                pltpu.make_async_copy(source, states_ref, sem).start()

        out_ref[...] = jnp.where(z == stages - 1, fresh_ref[...], arrived_ref[...])
        pltpu.make_async_copy(stored[0], states_ref, sem).wait()

        def layer(step, carry):
            index = 1 - step
            place = index ^ swap
            upstream = out_ref[...]
            upstream_ref[index] = upstream
            upstream_copy(index).start()
            moved, vgrad = backward_layer(
                upstream.astype(F32), states_ref[index].astype(F32), tv_ref.at[place], to_ref.at[place],
                sv_ref.at[place], so_ref.at[place], gain_ref[place])
            out_ref[...] = moved
            vgrad_ref[index] = vgrad
            vgrad_copy(index).start()
            return carry

        lax.fori_loop(0, 2, layer, 0)
        for index in range(2):
            upstream_copy(index).wait()
            vgrad_copy(index).wait()


def grads_kernel(micro, stages, ticks, info_ref, *rest):
    kinds = [rest[kind * ticks:(kind + 1) * ticks] for kind in range(4)]
    gv_ref, go_ref, uv_ref, uo_ref, up_ref, vg_ref, sems = rest[4 * ticks:]
    targets = (uv_ref, uo_ref, up_ref, vg_ref)
    z, swap = info_ref[0], info_ref[1]
    for place in range(stages):

        @pl.when(z == place)
        def _():
            for index in range(2):
                for kind, step in [(kind, step) for kind in (3, 0, 2, 1) for step in range(micro)]:
                    at = step + SKEW * (place if kind < 2 else stages - 1 - place)
                    pltpu.make_async_copy(
                        kinds[kind][at].at[index], targets[kind].at[index, step], sems.at[index, step, kind]).start()

    def arrive(index, chosen):
        for step in range(micro):
            for kind in chosen:
                pltpu.make_async_copy(
                    kinds[kind][0].at[index], targets[kind].at[index, step], sems.at[index, step, kind]).wait()

    for index in range(2):
        target = index ^ swap
        arrive(index, (0, 3))
        vgrads = [vg_ref[index, step].astype(F32) for step in range(micro)]

        def groups_v(block, carry):
            sums = []
            for at in range(8):
                total = uv_ref[index, 0, block * 8 + at].astype(F32) * vgrads[0]
                for step in range(1, micro):
                    total = total + uv_ref[index, step, block * 8 + at].astype(F32) * vgrads[step]
                sums.append(jnp.sum(total, axis=0, keepdims=True))
            gv_ref[target, pl.ds(pl.multiple_of(block * 8, 8), 8), :] = jnp.concatenate(sums, axis=0)
            return carry

        lax.fori_loop(0, gv_ref.shape[1] // 8, groups_v, 0)

        arrive(index, (1, 2))

        def cols_o(block, carry):
            cols = pl.ds(pl.multiple_of(block * 512, 512), 512)
            ups = [up_ref[index, step, :, cols].astype(F32) for step in range(micro)]
            sums = []
            for group in range(go_ref.shape[1]):
                total = uo_ref[index, 0, group, :, cols].astype(F32) * ups[0]
                for step in range(1, micro):
                    total = total + uo_ref[index, step, group, :, cols].astype(F32) * ups[step]
                sums.append(jnp.sum(total, axis=0, keepdims=True))
            go_ref[target, :, cols] = jnp.concatenate(sums, axis=0)
            return carry

        lax.fori_loop(0, go_ref.shape[2] // 512, cols_o, 0)


VMEM = pl.BlockSpec(memory_space=pltpu.VMEM)
SMEM = pl.BlockSpec(memory_space=pltpu.SMEM)
HBM = pl.BlockSpec(memory_space=pltpu.HBM)


def on_chip(value):
    return pltpu.with_memory_space_constraint(value, pltpu.VMEM)


def in_hbm(values):
    return [pltpu.with_memory_space_constraint(value, pltpu.HBM) for value in values]


def kernel_call(body, outs, in_specs, out_specs, scratch=(), aliases=None, flops=0, moved=0, name=None, vmem=VMEM_BYTES):
    return pl.pallas_call(
        body,
        out_shape=outs,
        in_specs=in_specs,
        out_specs=out_specs,
        scratch_shapes=list(scratch),
        input_output_aliases=aliases or {},
        compiler_params=pltpu.CompilerParams(vmem_limit_bytes=vmem),
        cost_estimate=pl.CostEstimate(flops=flops, bytes_accessed=moved, transcendentals=0),
        name=name,
    )


def fixed_swap(value, axis, bit):
    count = lax.axis_size(axis)
    return lax.ppermute(value, axis, [(source, source ^ bit) for source in range(count)])


def half_codes(words, core):
    low, high = jnp.split(words, 2, axis=1)
    return fixed_swap(jnp.where(core == 0, low, high), "section", 1)


def ends_rows(hidden_in, cotangent, stages):
    micro, rows, part = hidden_in.shape
    half = micro // 2
    hidden = hidden_in.reshape(2, half, rows, part).transpose(1, 0, 2, 3)
    last = cotangent.reshape(2, half, rows, part).transpose(1, 0, 2, 3)
    pieces = jnp.concatenate([hidden, last[::-1]]).reshape(4 * half, rows, part)
    found = lax.all_to_all(pieces, "section", 0, 0)
    found = found.transpose(1, 0, 2).reshape(rows, 4 * half * part)
    routes = []
    for place in range(1, half):
        for side_at in range(2):
            routes.append((2 * place + side_at, 2 * (place - 1) + side_at))
            routes.append((2 * (stages - 1 - place) + side_at, 2 * (stages - place) + side_at))
    ends = [found]
    for _ in range(half - 1):
        ends.append(lax.ppermute(ends[-1], "section", routes))
    return ends


def gather_steps(value):
    count = lax.axis_size("dp")
    return lax.all_to_all(jnp.broadcast_to(value[None], (count,) + value.shape), "dp", 0, 0)


def scatter_sums(value):
    total = value[0] + fixed_swap(value[1].astype(BF16), "section", 1).astype(F32)
    return jnp.sum(lax.all_to_all(total.astype(BF16), "dp", 0, 0).astype(F32), axis=0)


def on_device(hidden_in, cotangent, codes_v, zeros_v, steps_v, codes_o, zeros_o, steps_o, gain):
    section_id = lax.axis_index("section")
    section_count = lax.axis_size("section")
    dp_count = lax.axis_size("dp")
    z, side = section_id // 2, section_id % 2
    stages = section_count // 2
    micro = hidden_in.shape[0] // 2
    rows = hidden_in.shape[1]
    width, value_width = gain.shape[1], codes_v.shape[2]
    groups_v, groups_o = zeros_v.shape[1], zeros_o.shape[1]

    own_v = jnp.concatenate([pair_words(codes_v[0]), zeros_v[0]], axis=0)
    own_o = jnp.concatenate([pair_words(codes_o[0]), zeros_o[0]], axis=0)
    core = lax.axis_index("dp") % 2
    same_v, same_o = half_codes(own_v, core), half_codes(own_o, core)
    ends = ends_rows(hidden_in, cotangent, stages)
    count_v, count_o = steps_v.size, steps_o.size
    steps = gather_steps(jnp.concatenate([steps_v.reshape(-1), steps_o.reshape(-1)]).astype(BF16)).astype(F32)
    own_sv = steps[:, :count_v].reshape(dp_count, groups_v, -1).transpose(1, 0, 2).reshape(-1, width)
    own_so = steps[:, count_v:].reshape(dp_count, groups_o, -1).transpose(1, 0, 2).reshape(groups_o, width)
    own_steps = jnp.concatenate([own_sv, own_so, gain], axis=0)
    far_steps = fixed_swap(own_steps, "section", 1)
    order, unorder = order_matrices()
    info = jnp.stack([z, side, core]).astype(I32)
    own_v, own_o, own_steps, same_v, same_o, order, unorder, info, ends[0] = lax.optimization_barrier(
        (own_v, own_o, own_steps, same_v, same_o, order, unorder, info, ends[0]))
    other_v, other_o = fixed_swap(same_v, "dp", 1), fixed_swap(same_o, "dp", 1)

    q_shapes = (pltpu.VMEM((2, width, value_width), F8), pltpu.VMEM((2, value_width, width), F8))
    qv, qo = kernel_call(
        unpack_own_kernel, q_shapes, [VMEM] * 2, (VMEM, VMEM), flops=10**8, moved=2**22, name="unpack_own",
    )(own_v, own_o)
    qv, qo, sv, so, gains = kernel_call(
        unpack_far_kernel,
        q_shapes + tuple(jax.ShapeDtypeStruct(shape, F32) for shape in (
            (2, groups_v, value_width), (2, groups_o, width), (2, 1, width))),
        [SMEM] + [VMEM] * 8, (VMEM,) * 5, aliases={7: 0, 8: 1}, flops=10**8, moved=2**22, name="unpack_far",
    )(info, same_v, other_v, same_o, other_o, own_steps, far_steps, on_chip(qv), on_chip(qo))
    qv, qo = on_chip(qv), on_chip(qo)

    t_shapes = (pltpu.VMEM((2, value_width, width), F8), pltpu.VMEM((2, width, value_width), F8))
    turned = [None, None]

    def turn(which, late, place, unorder):
        body = (turn_v_kernel, turn_o_kernel)[which]
        known = [] if turned[which] is None else [on_chip(turned[which])]
        turned[which] = kernel_call(
            lambda *refs: body(late, place, *refs), t_shapes[which], [SMEM] + [VMEM] * (2 + len(known)), VMEM,
            aliases={3: 0} if known else {}, flops=10**8, moved=2**22, name="turn",
        )(info, unorder, (qv, qo)[which], *known)

    uv_shape, uo_shape = (2, groups_v, rows, value_width), (2, groups_o, rows, width)
    stored_shapes = [(2, rows, width), uv_shape, uo_shape]
    flops = 4 * 2 * rows * width * value_width * 2
    last = stages - 1
    ticks = micro + SKEW * last

    def forward(tick, arrived, info):
        done = kernel_call(
            lambda *refs: forward_kernel(tick, micro, *refs),
            (jax.ShapeDtypeStruct((rows, width), BF16),) + tuple(pltpu.HBM(shape, BF16) for shape in stored_shapes),
            [SMEM] + [VMEM] * 8, (VMEM, HBM, HBM, HBM),
            scratch=[pltpu.VMEM(shape, BF16) for shape in stored_shapes] + [pltpu.SemaphoreType.DMA((2, 3))],
            flops=flops, moved=2**24, name="forward",
        )(info, arrived, ends[min(tick, micro - 1)], qv, qo, sv, so, gains, order)
        return done[0], done[1:]

    def backward(tick, arrived, stored, info):
        places = [place for place in range(stages) if 0 <= tick - SKEW * (last - place) < micro]
        sources = [stored[SKEW * place + tick - SKEW * (last - place)][0] for place in places]
        return kernel_call(
            lambda *refs: backward_kernel(tick, micro, stages, places, *refs),
            (jax.ShapeDtypeStruct((rows, width), BF16), pltpu.HBM((2, rows, width), BF16),
             pltpu.HBM((2, rows, value_width), BF16)),
            [SMEM] + [VMEM] * 7 + [HBM] * len(places), (VMEM, HBM, HBM),
            scratch=[pltpu.VMEM((2, rows, width), BF16), pltpu.VMEM((2, rows, width), BF16),
                     pltpu.VMEM((2, rows, value_width), BF16), pltpu.SemaphoreType.DMA, pltpu.SemaphoreType.DMA((2, 2))],
            flops=flops, moved=2**24, name="backward",
        )(info, arrived, ends[min(tick, micro - 1)], on_chip(turned[0]), on_chip(turned[1]), sv, so, gains, *in_hbm(sources))

    up_routes = [(source, source + 2) for source in range(section_count - 2)]
    down_routes = [(source + 2, source) for source in range(section_count - 2)]
    empty = jnp.zeros((rows, width), BF16)
    sent_f, sent_b, stored, backs = [], [], [], []
    for tick in range(2 * ticks - micro + 1):
        if tick < ticks:
            out, kept = forward(tick, sent_f[tick - SKEW] if tick >= SKEW else empty, info)
            stored.append(kept)
            sent_f.append(lax.ppermute(out, "section", up_routes) if tick < ticks - SKEW else None)
            for first, late in ((1, True), (ticks - 7, False)):
                if 0 <= tick - first < 4:
                    which, place = divmod(tick - first, 2)
                    turn(which, late, place, lax.optimization_barrier((unorder, out))[0])
                    info, turned[which] = lax.optimization_barrier((info, turned[which]))
        back = tick - (ticks - micro + 1)
        if back >= 0:
            out, upstream, vgrad = backward(back, sent_b[back - SKEW] if back >= SKEW else empty, stored, info)
            backs.append((upstream, vgrad))
            sent_b.append(lax.ppermute(out, "section", down_routes) if back < ticks - SKEW else None)

    stored_all = [kept[1] for kept in stored] + [kept[2] for kept in stored]
    stored_all += [back[0] for back in backs] + [back[1] for back in backs]
    sums = kernel_call(
        lambda *refs: grads_kernel(micro, stages, ticks, *refs),
        (jax.ShapeDtypeStruct((2, groups_v, value_width), F32), jax.ShapeDtypeStruct((2, groups_o, width), F32)),
        [SMEM] + [HBM] * len(stored_all), (VMEM, VMEM),
        scratch=[pltpu.VMEM((2, micro) + shape, BF16) for shape in (uv_shape[1:], uo_shape[1:], (rows, width), (rows, value_width))]
        + [pltpu.SemaphoreType.DMA((2, micro, 4))],
        flops=10**7, moved=2**24, name="grads", vmem=24 * 2**20,
    )(info, *in_hbm(stored_all))

    total_v = sums[0].reshape(2, groups_v, dp_count, -1).transpose(0, 2, 1, 3).reshape(2, dp_count, -1)
    total_o = sums[1].reshape(2, groups_o, dp_count, -1).transpose(0, 2, 1, 3).reshape(2, dp_count, -1)
    total = scatter_sums(jnp.concatenate([total_v, total_o], axis=2))
    return total[:count_v].reshape(steps_v.shape), total[count_v:].reshape(steps_o.shape)


def solution(mesh):
    return jax.shard_map(
        on_device,
        mesh=mesh,
        in_specs=(
            P(None, "dp", "section"),
            P(None, "dp", "section"),
            P("section", None, None),
            P("section", None, None),
            P("section", None, "dp"),
            P("section", None, None),
            P("section", None, None),
            P("section", None, "dp"),
            P("section", None),
        ),
        out_specs=(P("section", None, "dp"), P("section", None, "dp")),
        check_vma=False,
    )
```
